32 devices in a mesh: groups: 2 (over y), gz: 4 (over z), gy: 2 (over x), gx: 2 (over core).
Axes of the slice: x: 2, y: 2, z: 4, core: 2. Of those that a mesh axis runs over, the one named last changes fastest.
Arguments:
- populations: float32 [19, 32, 32, 512], P(None, ('groups', 'gx'), 'gy', 'gz'), parts along dimension 1, as said below
- displacement: float32 [3, 164352], P(None, ('groups', 'gz', 'gy', 'gx')), parts along dimension 1, may hold values from -0.18 to 0.18
- stiffness: float32 [256], P(('groups', 'gz', 'gy', 'gx')), parts along dimension 0, may hold values from 0.5 to 8
- base_node: int32 [3, 164352], P(None, ('groups', 'gz', 'gy', 'gx')), parts along dimension 1, may hold values from 1 to 124, as said below
- offset: float32 [3, 164352], P(None, ('groups', 'gz', 'gy', 'gx')), parts along dimension 1, may hold values from 0 to 1
- destination: int32 [164352, 1], P(('groups', 'gz', 'gy', 'gx')), parts along dimension 0, may hold values from 0 to 7; in each aligned block of 5136 rows (0 to 5135, 5136 to 10271, ...) at most 1284 rows name the same one
Outputs:
- new_populations: float32 [19, 32, 32, 512], P(None, ('groups', 'gx'), 'gy', 'gz'), parts along dimension 1
- marker_velocity: float32 [3, 164352], P(None, ('groups', 'gz', 'gy', 'gx')), parts along dimension 1
The draws below stay inside these ranges and needn't reach their ends.
There are 2 independent parts, one for each index of `groups`. The reference program is written for one: setup_inputs(seed, part) draws one part's arguments, and reference() takes and returns one part's arrays. A program takes and returns all parts, laid end to end along the dimension named above; each array names one. Nothing has to cross between parts.
Inputs may be any that keep to these rules, and one draw needn't show every extreme that they name: `base_node`: row 0 lies in 1 .. 4, row 1 in 1 .. 12, row 2 in 1 .. 124, so that every kernel node lies in the destination brick. The rows of one device name each destination at most 1284 times; in every draw some device names some destination exactly 1284 times. `populations`: every population lies between one half and one and a half times its lattice weight.
All inputs are finite; a program needn't handle non-finite values.
Results may differ from the reference program's by a relative error of at most 0.0003.
Values sent between devices are 32-bit elements; how exact they have to be, the bound alone decides.
A program may use at most 64 MiB of HBM per device.

```python
import math
import jax
import jax.numpy as jnp
import numpy as np

CX = 8
CY = 16
CZ = 128
MK_DEV = 5136
CAP = 1284
CELLS = 128
MARKERS = 82176
NX = 16
NY = 32
NZ = 512
N_GZ = 4
N_GY = 2
N_GX = 2


LATTICE_WEIGHTS = [1.0 / 3.0] + [1.0 / 18.0] * 6 + [1.0 / 36.0] * 12


def draw_populations(key, part):
    key = jax.random.fold_in(key, 11)
    weights = jnp.array(LATTICE_WEIGHTS, jnp.float32)[:, None, None, None]
    noise = jax.random.uniform(key, (19, NX, NY, NZ), jnp.float32, 0.7, 1.3)
    return weights * noise


def draw_base_node(key, part):
    key = jax.random.fold_in(key, 23)
    first_key, second_key, third_key = jax.random.split(key, 3)
    row_x = jax.random.randint(first_key, (MARKERS,), 1, CX - 3, dtype=jnp.int32)
    row_y = jax.random.randint(second_key, (MARKERS,), 1, CY - 3, dtype=jnp.int32)
    row_z = jax.random.randint(third_key, (MARKERS,), 1, CZ - 3, dtype=jnp.int32)
    return jnp.stack([row_x, row_y, row_z])


def steps_of(key, extent, cuts, least, largest):
    def one(axis_at, shards_of):
        steps = jax.random.uniform(jax.random.fold_in(jax.random.fold_in(key, 6), axis_at), (shards_of,), jnp.float32, least / len(cuts), largest / len(cuts))
        return jnp.repeat(jnp.exp(steps), extent[axis_at] // shards_of).reshape((-1,) + (1,) * (len(extent) - axis_at - 1))

    level = one(*cuts[0])
    for cut in cuts[1:]:
        level = level * one(*cut)
    return level


def routed_block(stream_key, own, number, rows, number_of, top, bound, skew):
    ranking = jax.random.permutation(stream_key, number_of)
    packed, common = shares(number_of, rows * top, bound, skew, True), shares(number_of, rows * top, bound, skew, False)
    places = jnp.arange(number_of)

    def named(sizes, turn):
        used = int((sizes > 0).sum())
        fixed = max(1, used // 4)
        passed = fixed + (places - fixed + turn * (used - fixed)) % max(1, number_of - fixed)
        return jnp.zeros((number_of,), jnp.int32).at[ranking[jnp.where(places < fixed, places, passed)]].set(jnp.asarray(sizes, jnp.int32))

    sizes = jnp.where(number % 4 == 0, named(packed, number // 4), named(common, number - number // 4 - 1))
    mixed = jax.random.permutation(jax.random.fold_in(own, 3), number_of)
    source_of, sink = mixed[0:number_of // 2 * 2:2], mixed[1:number_of // 2 * 2:2]
    margin = jnp.minimum(sizes[source_of] - 1, bound - sizes[sink]) // 2
    margin = jnp.where((source_of == ranking[0]) | (sink == ranking[0]) | (sizes[sink] == 0), 0, jnp.maximum(margin, 0))
    passed = jax.random.randint(jax.random.fold_in(own, 4), (number_of // 2,), 0, 1 << 20) % (margin + 1)
    sizes = sizes.at[source_of].add(-passed).at[sink].add(passed)
    items = jnp.searchsorted(jnp.cumsum(sizes), jnp.arange(rows * top), side="right").astype(jnp.int32)
    listing = items.reshape(top, rows).T
    listing = listing[jax.random.permutation(jax.random.fold_in(own, 1), rows)]
    turn = jax.random.randint(jax.random.fold_in(own, 2), (rows, 1), 0, top)
    return jnp.take_along_axis(listing, (jnp.arange(top)[None, :] + turn) % top, axis=1)


def shares(number_of, total, limit, slope, full):
    loads = [(1 << 20) // math.isqrt(rank ** slope) + 1 for rank in range(1, number_of + 1)]
    largest = limit if full else min(limit, max(-(-total // number_of), total * loads[0] // sum(loads)))
    least = 1 if total - largest >= number_of - 1 else 0
    given, surplus = [largest] + [least] * (number_of - 1), total - largest - least * (number_of - 1)
    while surplus > 0:
        movable = [i for i in range(1, number_of) if given[i] < largest] or [i for i in range(1, number_of) if given[i] < limit]
        mass, remaining = sum([loads[i] for i in movable]), surplus
        for i in movable:
            more = min(limit - given[i], max(1, remaining * loads[i] // mass), surplus)
            given[i] = given[i] + more
            surplus = surplus - more
    return np.array(given)


def scatter_about(rng, dims, width, bound, cuts=(), kind=jnp.bfloat16):
    values = width * jax.random.normal(rng, dims, jnp.float32)
    if cuts:
        values = values * steps_of(rng, dims, cuts, -0.22, 0.18)
    return jnp.clip(values, -bound, bound).astype(kind)


def setup_inputs(seed: int = 0, part: int = 0) -> dict:
    keys = jax.random.split(jax.random.key(seed), 7)
    part_splits = jax.random.split(jax.random.fold_in(keys[6], part), 7)
    populations = draw_populations(jax.random.fold_in(jax.random.fold_in(keys[6], part), 71), part)
    displacement = scatter_about(part_splits[1], (3, MARKERS), 0.03, 0.18, ((1, 16),), jnp.float32)
    stiffness = jnp.clip(jnp.exp(math.log(8.0) - 2.7725887 * jax.random.uniform(part_splits[2], (CELLS,), jnp.float32) ** steps_of(part_splits[2], (CELLS,), ((0, 16),), -0.2, 0.2)), 0.5, 8.0)
    base_node = draw_base_node(jax.random.fold_in(jax.random.fold_in(keys[6], part), 71), part)
    offset = jnp.clip(1.0 * jax.random.uniform(part_splits[4], (3, MARKERS), jnp.float32) ** steps_of(part_splits[4], (3, MARKERS), ((1, 16),), -0.2, 0.2), 0.0, 1.0)
    destination_keys = jax.random.split(jax.random.fold_in(part_splits[5], 1), MARKERS // MK_DEV)
    destination_turns = jax.random.permutation(jax.random.fold_in(part_splits[5], 3), MARKERS // MK_DEV)
    destination = jax.vmap(lambda own, number: routed_block(jax.random.fold_in(part_splits[5], 2), own, number, MK_DEV, N_GZ * N_GY, 1, CAP, 2))(destination_keys, destination_turns).reshape((MARKERS, 1))
    return dict(populations=populations, displacement=displacement, stiffness=stiffness, base_node=base_node, offset=offset, destination=destination)


LATTICE = np.array([[0, 0, 0], [1, 0, 0], [-1, 0, 0], [0, 1, 0], [0, -1, 0], [0, 0, 1], [0, 0, -1],
                    [1, 1, 0], [-1, -1, 0], [1, -1, 0], [-1, 1, 0], [1, 0, 1], [-1, 0, -1], [1, 0, -1],
                    [-1, 0, 1], [0, 1, 1], [0, -1, -1], [0, 1, -1], [0, -1, 1]])
WEIGHTS = [1.0 / 3.0] + [1.0 / 18.0] * 6 + [1.0 / 36.0] * 12
RELAXATION = 0.8
VELOCITY_UNIT = 0.01


def kernel(distance):
    return jnp.where(jnp.abs(distance) < 2.0, 0.25 * (1.0 + jnp.cos(0.5 * math.pi * distance)), 0.0)


def marker_forces(displacement, stiffness):
    grouped = displacement.reshape(3, stiffness.shape[0], -1)
    centred = grouped - jnp.mean(grouped, axis=2, keepdims=True)
    return (stiffness[None, :, None] * centred).reshape(3, -1)


def momentum_sum(populations, dimension):
    total = jnp.zeros_like(populations[0])
    for index in range(19):
        step_sign = int(LATTICE[index][dimension])
        if step_sign != 0:
            total = total + step_sign * populations[index]
    return total


def collide(populations, force_field):
    density = jnp.sum(populations, axis=0)
    velocity = [(momentum_sum(populations, dimension) + 0.5 * force_field[dimension]) / density for dimension in range(3)]
    speed_squared = velocity[0] * velocity[0] + velocity[1] * velocity[1] + velocity[2] * velocity[2]
    factor = 1.0 - 0.5 / RELAXATION
    result = []
    for index in range(19):
        lattice_row = [int(value) for value in LATTICE[index]]
        along = jnp.zeros_like(density)
        for dimension in range(3):
            if lattice_row[dimension] != 0:
                along = along + lattice_row[dimension] * velocity[dimension]
        equilibrium = WEIGHTS[index] * density * (1.0 + 3.0 * along + 4.5 * along * along - 1.5 * speed_squared)
        source = jnp.zeros_like(density)
        for dimension in range(3):
            source = source + (3.0 * (lattice_row[dimension] - velocity[dimension]) + 9.0 * along * lattice_row[dimension]) * force_field[dimension]
        result.append(populations[index] - (populations[index] - equilibrium) / RELAXATION + factor * WEIGHTS[index] * source)
    return jnp.stack(result)


def fluid_velocity(populations):
    density = jnp.sum(populations, axis=0)
    return jnp.stack([momentum_sum(populations, dimension) / density for dimension in range(3)])


def reference(populations, displacement, stiffness, base_node, offset, destination):
    size_x, size_y, size_z = populations.shape[1], populations.shape[2], populations.shape[3]
    forces = marker_forces(displacement, stiffness)
    position = base_node.astype(jnp.float32) + offset
    marker_count = displacement.shape[1]
    device = jnp.arange(marker_count, dtype=jnp.int32) // MK_DEV
    target = destination[:, 0]
    corner = [(device % N_GX) * CX, (target % N_GY) * CY, (target // N_GY) * CZ]
    shifts = jnp.arange(-1, 3, dtype=jnp.int32)
    node_index = []
    node_weight = []
    for dimension in range(3):
        local = base_node[dimension][:, None] + shifts[None, :]
        node_weight.append(kernel(local.astype(jnp.float32) - position[dimension][:, None]))
        node_index.append((corner[dimension][:, None] + local).astype(jnp.int32))
    force_field = jnp.zeros((3, size_x * size_y * size_z), jnp.float32)
    stencil = []
    for step_x in range(4):
        for step_y in range(4):
            for step_z in range(4):
                flat_index = (node_index[0][:, step_x] * size_y + node_index[1][:, step_y]) * size_z + node_index[2][:, step_z]
                weight = node_weight[0][:, step_x] * node_weight[1][:, step_y] * node_weight[2][:, step_z]
                stencil.append((flat_index, weight))
                force_field = force_field.at[:, flat_index].add(forces * weight[None, :])
    force_field = force_field.reshape(3, size_x, size_y, size_z)
    post = collide(populations, force_field)
    read = []
    for index in range(19):
        lattice_row = [int(value) for value in LATTICE[index]]
        read.append(jnp.roll(post[index], shift=(lattice_row[0], lattice_row[1], lattice_row[2]), axis=(0, 1, 2)))
    new_populations = jnp.stack(read)
    flat_velocity = fluid_velocity(new_populations).reshape(3, -1)
    sampled = jnp.zeros((3, marker_count), jnp.float32)
    for flat_index, weight in stencil:
        sampled = sampled + flat_velocity[:, flat_index] * weight[None, :]
    return new_populations, sampled / VELOCITY_UNIT
```

```python
import math

import jax
import jax.numpy as jnp
import numpy as np
from jax import lax
from jax.experimental import pallas as pl
from jax.experimental.pallas import tpu as pltpu
from jax.sharding import PartitionSpec as P

LATTICE = np.array(
    [
        [0, 0, 0],
        [1, 0, 0],
        [-1, 0, 0],
        [0, 1, 0],
        [0, -1, 0],
        [0, 0, 1],
        [0, 0, -1],
        [1, 1, 0],
        [-1, -1, 0],
        [1, -1, 0],
        [-1, 1, 0],
        [1, 0, 1],
        [-1, 0, -1],
        [1, 0, -1],
        [-1, 0, 1],
        [0, 1, 1],
        [0, -1, -1],
        [0, 1, -1],
        [0, -1, 1],
    ]
)
WEIGHTS = [1.0 / 3.0] + [1.0 / 18.0] * 6 + [1.0 / 36.0] * 12
RELAXATION = 0.8
VELOCITY_UNIT = 0.01


def padded_2(shard, sides, width):
    for axis, dim in sides:
        size, length = (lax.axis_size(axis), shard.shape[dim])
        up = [(i, (i + 1) % size) for i in range(size)]
        down = [(j, i) for i, j in up]
        last = lax.slice_in_dim(shard, length - width, length, axis=dim)
        initial = lax.slice_in_dim(shard, 0, width, axis=dim)
        before = lax.ppermute(last, axis, up)
        after = lax.ppermute(initial, axis, down)
        shard = jnp.concatenate([before, shard, after], axis=dim)
    return shard


def marker_forces(displacement, stiffness):
    grouped = displacement.reshape(3, stiffness.shape[0], -1)
    centred = grouped - jnp.mean(grouped, axis=2, keepdims=True)
    return (stiffness[None, :, None] * centred).reshape(3, -1)


def momentum_sum(populations, dimension):
    total = jnp.zeros_like(populations[0])
    for index in range(19):
        step_sign = int(LATTICE[index][dimension])
        if step_sign != 0:
            total = total + step_sign * populations[index]
    return total


def collide(populations, force_field):
    density = jnp.sum(populations, axis=0)
    velocity = [
        (momentum_sum(populations, dimension) + 0.5 * force_field[dimension]) / density
        for dimension in range(3)
    ]
    speed_squared = (
        velocity[0] * velocity[0] + velocity[1] * velocity[1] + velocity[2] * velocity[2]
    )
    factor = 1.0 - 0.5 / RELAXATION
    result = []
    for index in range(19):
        lattice_row = [int(value) for value in LATTICE[index]]
        along = jnp.zeros_like(density)
        for dimension in range(3):
            if lattice_row[dimension] != 0:
                along = along + lattice_row[dimension] * velocity[dimension]
        equilibrium = (
            WEIGHTS[index]
            * density
            * (1.0 + 3.0 * along + 4.5 * along * along - 1.5 * speed_squared)
        )
        source = jnp.zeros_like(density)
        for dimension in range(3):
            source = (
                source
                + (
                    3.0 * (lattice_row[dimension] - velocity[dimension])
                    + 9.0 * along * lattice_row[dimension]
                )
                * force_field[dimension]
            )
        result.append(
            populations[index]
            - (populations[index] - equilibrium) / RELAXATION
            + factor * WEIGHTS[index] * source
        )
    return jnp.stack(result)


def fluid_velocity(populations):
    density = jnp.sum(populations, axis=0)
    return jnp.stack([momentum_sum(populations, dimension) / density for dimension in range(3)])


LANES = 128
VMEM_LIMIT = 48 * 1024 * 1024
NT = (((1,), (1,)), ((), ()))
NN = (((1,), (0,)), ((), ()))


def iota(shape, dimension):
    return lax.broadcasted_iota(jnp.int32, shape, dimension)


def split_two(value):
    high = value.astype(jnp.bfloat16)
    return high, (value - high.astype(jnp.float32)).astype(jnp.bfloat16)


def route_kernel(peers, rows, target_ref, payload_ref, sent_ref, slot_ref, left_ref, right_ref):
    chunks = target_ref.shape[0]
    target = target_ref[...]
    bf16 = jnp.bfloat16
    upper = (iota((LANES, LANES), 0) < iota((LANES, LANES), 1)).astype(bf16)
    lower = (iota((chunks, chunks), 1) < iota((chunks, chunks), 0)).astype(bf16)
    ones = jnp.ones((LANES, LANES), bf16)

    def ranked(peer, rank):
        mask = target == peer
        onehot = mask.astype(jnp.float32).astype(bf16)
        within = lax.dot_general(onehot, upper, NN, preferred_element_type=jnp.float32)
        ahead = lax.dot_general(lower, onehot, NN, preferred_element_type=jnp.float32)
        before = lax.dot_general(ahead.astype(bf16), ones, NN, preferred_element_type=jnp.float32)
        return jnp.where(mask, within + before, rank)

    rank = lax.fori_loop(0, peers, ranked, jnp.zeros(target.shape, jnp.float32)).astype(jnp.int32)
    slot_ref[0] = jnp.where(target < 0, -1, target * rows + lax.div(rank, LANES))
    slot_ref[1] = lax.rem(rank, LANES)
    height = left_ref.shape[0] // 15

    def place(chunk, carry):
        at = pl.ds(pl.multiple_of(chunk * LANES, LANES), LANES)
        high_mask = iota((height, LANES), 0) == slot_ref[0, pl.ds(chunk, 1), :]
        low_mask = iota((LANES, LANES), 0) == slot_ref[1, pl.ds(chunk, 1), :]
        right_ref[:, at] = low_mask.astype(jnp.float32).astype(bf16)
        values = payload_ref[:, at]
        first = values.astype(bf16).astype(jnp.float32)
        rest = values - first
        second = rest.astype(bf16).astype(jnp.float32)
        third = rest - second
        piece = 0
        for row in range(6):
            for part in (first, second, third)[: 2 if row < 3 else 3]:
                left_ref[piece * height : (piece + 1) * height, at] = jnp.where(
                    high_mask, part[row : row + 1, :], 0.0
                ).astype(bf16)
                piece += 1
        return carry

    lax.fori_loop(0, chunks, place, 0)
    placed = lax.dot_general(
        left_ref[...], right_ref[...], NT, preferred_element_type=jnp.float32
    )
    piece = 0
    for row in range(6):
        count = 2 if row < 3 else 3
        total = placed[piece * height : (piece + 1) * height]
        for more in range(1, count):
            total = total + placed[(piece + more) * height : (piece + more + 1) * height]
        piece += count
        for peer in range(peers):
            sent_ref[peer, row * rows : (row + 1) * rows, :] = total[peer * rows : (peer + 1) * rows]


def route(target, payload, peers, rows):
    chunks = target.shape[0]
    height = -(-peers * rows // 16) * 16
    return pl.pallas_call(
        lambda *refs: route_kernel(peers, rows, *refs),
        out_shape=(
            jax.ShapeDtypeStruct((peers, 6 * rows, LANES), jnp.float32),
            jax.ShapeDtypeStruct((2, chunks, LANES), jnp.int32),
        ),
        scratch_shapes=[
            pltpu.VMEM((15 * height, chunks * LANES), jnp.bfloat16),
            pltpu.VMEM((LANES, chunks * LANES), jnp.bfloat16),
        ],
        compiler_params=pltpu.CompilerParams(vmem_limit_bytes=VMEM_LIMIT),
        name="route",
    )(target, payload)


def stencil(position):
    base = jnp.floor(position)
    angle = (0.5 * math.pi) * (position - base)
    sine, cosine = jnp.sin(angle), jnp.cos(angle)
    weights = [0.25 - 0.25 * sine, 0.25 + 0.25 * cosine, 0.25 + 0.25 * sine, 0.25 - 0.25 * cosine]
    return base.astype(jnp.int32), weights


def node_weights(size, base, weights, row):
    step = iota((size, LANES), 0) - base[row : row + 1, :]
    result = jnp.zeros((size, LANES), jnp.float32)
    for index in range(4):
        result = jnp.where(step == index - 1, weights[index][row : row + 1, :], result)
    return result


def spread_kernel(sizes, rows, arrived_ref, field_ref, left_ref, right_ref, total_ref):
    size_x, size_y, size_z = sizes
    height = 3 * size_x * size_y
    total_ref[...] = jnp.zeros_like(total_ref)

    def one(peer, carry):
        block = arrived_ref[peer]
        base, weights = stencil(block[3 * rows : 6 * rows])
        for k in range(rows):
            at = slice(k * LANES, (k + 1) * LANES)
            along_x = node_weights(size_x, base, weights, k)
            along_y = node_weights(size_y, base, weights, rows + k)
            high, low = split_two(node_weights(size_z, base, weights, 2 * rows + k))
            right_ref[:size_z, at] = high
            right_ref[size_z:, at] = low
            for dimension in range(3):
                scaled = along_x * block[dimension * rows + k : dimension * rows + k + 1, :]
                for x in range(size_x):
                    first = (dimension * size_x + x) * size_y
                    high, low = split_two(along_y * scaled[x : x + 1, :])
                    left_ref[first : first + size_y, at] = high
                    left_ref[height + first : height + first + size_y, at] = low
        total_ref[...] += lax.dot_general(
            left_ref[...], right_ref[...], NT, preferred_element_type=jnp.float32
        )
        return carry

    lax.fori_loop(0, arrived_ref.shape[0], one, 0)
    field_ref[...] = (total_ref[height:, size_z:] + total_ref[height:, :size_z]) + (
        total_ref[:height, size_z:] + total_ref[:height, :size_z]
    )


def spread(arrived, sizes, rows):
    height = 3 * sizes[0] * sizes[1]
    return pl.pallas_call(
        lambda *refs: spread_kernel(sizes, rows, *refs),
        out_shape=jax.ShapeDtypeStruct((height, sizes[2]), jnp.float32),
        scratch_shapes=[
            pltpu.VMEM((2 * height, rows * LANES), jnp.bfloat16),
            pltpu.VMEM((2 * sizes[2], rows * LANES), jnp.bfloat16),
            pltpu.VMEM((2 * height, 2 * sizes[2]), jnp.float32),
        ],
        compiler_params=pltpu.CompilerParams(vmem_limit_bytes=VMEM_LIMIT),
        name="spread",
    )(arrived)


def sample_kernel(sizes, rows, arrived_ref, velocity_ref, sampled_ref, left_ref, right_ref, part_ref):
    size_x, size_y, size_z = sizes
    high, low = split_two(velocity_ref[...])
    left_ref[:, :size_z] = high
    left_ref[:, size_z : 2 * size_z] = low
    left_ref[:, 2 * size_z :] = high

    def one(peer, carry):
        base, weights = stencil(arrived_ref[peer, 3 * rows : 6 * rows, :])
        for k in range(rows):
            at = slice(k * LANES, (k + 1) * LANES)
            high, low = split_two(node_weights(size_z, base, weights, 2 * rows + k))
            right_ref[:size_z, at] = high
            right_ref[size_z : 2 * size_z, at] = high
            right_ref[2 * size_z :, at] = low
        part_ref[...] = lax.dot_general(
            left_ref[...], right_ref[...], NN, preferred_element_type=jnp.float32
        )
        for k in range(rows):
            at = slice(k * LANES, (k + 1) * LANES)
            along_x = node_weights(size_x, base, weights, k)
            along_y = node_weights(size_y, base, weights, rows + k)
            for dimension in range(3):
                total = jnp.zeros((size_y, LANES), jnp.float32)
                for x in range(size_x):
                    first = (dimension * size_x + x) * size_y
                    total = total + along_x[x : x + 1, :] * part_ref[first : first + size_y, at]
                across = jnp.sum(total * along_y, axis=0, keepdims=True)
                sampled_ref[peer, dimension * rows + k : dimension * rows + k + 1, :] = (
                    across / VELOCITY_UNIT
                )
        return carry

    lax.fori_loop(0, arrived_ref.shape[0], one, 0)


def sample(arrived, velocity, sizes, rows):
    height = 3 * sizes[0] * sizes[1]
    peers = arrived.shape[0]
    return pl.pallas_call(
        lambda *refs: sample_kernel(sizes, rows, *refs),
        out_shape=jax.ShapeDtypeStruct((peers, 3 * rows, LANES), jnp.float32),
        scratch_shapes=[
            pltpu.VMEM((height, 3 * sizes[2]), jnp.bfloat16),
            pltpu.VMEM((3 * sizes[2], rows * LANES), jnp.bfloat16),
            pltpu.VMEM((height, rows * LANES), jnp.float32),
        ],
        compiler_params=pltpu.CompilerParams(vmem_limit_bytes=VMEM_LIMIT),
        name="sample",
    )(arrived, velocity)


def collect_kernel(peers, rows, returned_ref, slot_ref, result_ref, table_ref, left_ref):
    height = left_ref.shape[0] // 3
    markers = result_ref.shape[1]
    table_ref[...] = jnp.zeros_like(table_ref)
    for row in range(3):
        for peer in range(peers):
            first = row * height + peer * rows
            table_ref[first : first + rows, :] = returned_ref[peer, row * rows : (row + 1) * rows, :]
    high, low = split_two(table_ref[...])
    left_ref[:, :LANES] = high
    left_ref[:, LANES:] = low

    def one(chunk, width):
        low_mask = iota((LANES, LANES), 0) == slot_ref[1, pl.ds(chunk, 1), :]
        onehot = low_mask.astype(jnp.float32).astype(jnp.bfloat16)
        found = lax.dot_general(
            left_ref[...],
            jnp.concatenate([onehot, onehot], axis=0),
            NN,
            preferred_element_type=jnp.float32,
        )
        high_mask = iota((height, LANES), 0) == slot_ref[0, pl.ds(chunk, 1), :]
        values = jnp.concatenate(
            [
                jnp.sum(
                    jnp.where(high_mask, found[row * height : (row + 1) * height], 0.0),
                    axis=0,
                    keepdims=True,
                )
                for row in range(3)
            ],
            axis=0,
        )
        if width == LANES:
            result_ref[:, pl.ds(pl.multiple_of(chunk * LANES, LANES), LANES)] = values
        else:
            result_ref[:, markers - width :] = values[:, :width]

    whole = markers // LANES

    def step(chunk, carry):
        one(chunk, LANES)
        return carry

    lax.fori_loop(0, whole, step, 0, unroll=4)
    if markers % LANES:
        one(whole, markers % LANES)


def collect(returned, slots, markers, peers, rows):
    height = -(-peers * rows // 16) * 16
    return pl.pallas_call(
        lambda *refs: collect_kernel(peers, rows, *refs),
        out_shape=jax.ShapeDtypeStruct((3, markers), jnp.float32),
        scratch_shapes=[
            pltpu.VMEM((3 * height, LANES), jnp.float32),
            pltpu.VMEM((3 * height, 2 * LANES), jnp.bfloat16),
        ],
        compiler_params=pltpu.CompilerParams(vmem_limit_bytes=VMEM_LIMIT),
        name="collect",
    )(returned, slots)


def moving_rows(dimension):
    return [index for index in range(19) if int(LATTICE[index][dimension]) != 0]


def shift_along(field, padded, moving, dimension, length):
    pieces = [field[index] for index in range(19)]
    for slot_pos, index in enumerate(moving):
        first_cell = 1 - int(LATTICE[index][dimension])
        pieces[index] = lax.slice_in_dim(
            padded[slot_pos], first_cell, first_cell + length, axis=dimension
        )
    return jnp.stack(pieces)


def shards(populations, displacement, stiffness, base_node, offset, destination):
    size_x, size_y, size_z = (populations.shape[1], populations.shape[2], populations.shape[3])
    peer_count = lax.axis_size(("gz", "gy"))
    markers = displacement.shape[1]
    capacity = max(2, (2 * markers + peer_count - 1) // peer_count)
    rows = -(-capacity // LANES)
    chunks = -(-markers // LANES)
    spare = chunks * LANES - markers
    sizes = (size_x, size_y, size_z)
    forces = marker_forces(displacement, stiffness)
    position = base_node.astype(jnp.float32) + offset
    target = jnp.pad(destination[:, 0], (0, spare), constant_values=-1).reshape(chunks, LANES)
    payload = jnp.pad(jnp.concatenate([forces, position], axis=0), ((0, 0), (0, spare)))
    outgoing, slots = route(target, payload, peer_count, rows)
    arrived = lax.all_to_all(outgoing, ("gz", "gy"), split_axis=0, concat_axis=0, tiled=True)
    force_field = spread(arrived, sizes, rows).reshape(3, size_x, size_y, size_z)
    post = collide(populations, force_field)
    moving = moving_rows(0)
    padded = padded_2(jnp.stack([post[index] for index in moving]), (("gx", 1),), 1)
    post = shift_along(post, padded, moving, 0, size_x)
    moving = moving_rows(1)
    padded = padded_2(jnp.stack([post[index] for index in moving]), (("gy", 2),), 1)
    post = shift_along(post, padded, moving, 1, size_y)
    moving = moving_rows(2)
    padded = padded_2(jnp.stack([post[index] for index in moving]), (("gz", 3),), 1)
    new_populations = shift_along(post, padded, moving, 2, size_z)
    velocity = fluid_velocity(new_populations).reshape(3 * size_x * size_y, size_z)
    sampled = sample(arrived, velocity, sizes, rows)
    returned = lax.all_to_all(sampled, ("gz", "gy"), split_axis=0, concat_axis=0, tiled=True)
    marker_velocity = collect(returned, slots, markers, peer_count, rows)
    return (new_populations, marker_velocity)


def solution(mesh):
    return jax.shard_map(
        shards,
        mesh=mesh,
        in_specs=(
            P(None, ("groups", "gx"), "gy", "gz"),
            P(None, ("groups", "gz", "gy", "gx")),
            P(("groups", "gz", "gy", "gx")),
            P(None, ("groups", "gz", "gy", "gx")),
            P(None, ("groups", "gz", "gy", "gx")),
            P(("groups", "gz", "gy", "gx"), None),
        ),
        out_specs=(P(None, ("groups", "gx"), "gy", "gz"), P(None, ("groups", "gz", "gy", "gx"))),
        check_vma=False,
    )
```

```python
import math

import jax
import jax.numpy as jnp
import numpy as np
from jax import lax
from jax.experimental import pallas as pl
from jax.experimental.pallas import tpu as pltpu
from jax.sharding import PartitionSpec as P

LATTICE = np.array(
    [
        [0, 0, 0],
        [1, 0, 0],
        [-1, 0, 0],
        [0, 1, 0],
        [0, -1, 0],
        [0, 0, 1],
        [0, 0, -1],
        [1, 1, 0],
        [-1, -1, 0],
        [1, -1, 0],
        [-1, 1, 0],
        [1, 0, 1],
        [-1, 0, -1],
        [1, 0, -1],
        [-1, 0, 1],
        [0, 1, 1],
        [0, -1, -1],
        [0, 1, -1],
        [0, -1, 1],
    ]
)
WEIGHTS = [1.0 / 3.0] + [1.0 / 18.0] * 6 + [1.0 / 36.0] * 12
RELAXATION = 0.8
VELOCITY_UNIT = 0.01


def padded_2(shard, sides, width):
    for axis, dim in sides:
        size, length = (lax.axis_size(axis), shard.shape[dim])
        up = [(i, (i + 1) % size) for i in range(size)]
        down = [(j, i) for i, j in up]
        last = lax.slice_in_dim(shard, length - width, length, axis=dim)
        initial = lax.slice_in_dim(shard, 0, width, axis=dim)
        before = lax.ppermute(last, axis, up)
        after = lax.ppermute(initial, axis, down)
        shard = jnp.concatenate([before, shard, after], axis=dim)
    return shard


def marker_forces(displacement, stiffness):
    grouped = displacement.reshape(3, stiffness.shape[0], -1)
    centred = grouped - jnp.mean(grouped, axis=2, keepdims=True)
    return (stiffness[None, :, None] * centred).reshape(3, -1)


def momentum_sum(populations, dimension):
    total = jnp.zeros_like(populations[0])
    for index in range(19):
        step_sign = int(LATTICE[index][dimension])
        if step_sign != 0:
            total = total + step_sign * populations[index]
    return total


def collide(populations, force_field):
    density = jnp.sum(populations, axis=0)
    velocity = [
        (momentum_sum(populations, dimension) + 0.5 * force_field[dimension]) / density
        for dimension in range(3)
    ]
    speed_squared = (
        velocity[0] * velocity[0] + velocity[1] * velocity[1] + velocity[2] * velocity[2]
    )
    factor = 1.0 - 0.5 / RELAXATION
    result = []
    for index in range(19):
        lattice_row = [int(value) for value in LATTICE[index]]
        along = jnp.zeros_like(density)
        for dimension in range(3):
            if lattice_row[dimension] != 0:
                along = along + lattice_row[dimension] * velocity[dimension]
        equilibrium = (
            WEIGHTS[index]
            * density
            * (1.0 + 3.0 * along + 4.5 * along * along - 1.5 * speed_squared)
        )
        source = jnp.zeros_like(density)
        for dimension in range(3):
            source = (
                source
                + (
                    3.0 * (lattice_row[dimension] - velocity[dimension])
                    + 9.0 * along * lattice_row[dimension]
                )
                * force_field[dimension]
            )
        result.append(
            populations[index]
            - (populations[index] - equilibrium) / RELAXATION
            + factor * WEIGHTS[index] * source
        )
    return jnp.stack(result)


def fluid_velocity(populations):
    density = jnp.sum(populations, axis=0)
    return jnp.stack([momentum_sum(populations, dimension) / density for dimension in range(3)])


LANES = 128
VMEM_LIMIT = 48 * 1024 * 1024
NT = (((1,), (1,)), ((), ()))
NN = (((1,), (0,)), ((), ()))


def iota(shape, dimension):
    return lax.broadcasted_iota(jnp.int32, shape, dimension)


def split_two(value):
    high = value.astype(jnp.bfloat16)
    return high, (value - high.astype(jnp.float32)).astype(jnp.bfloat16)


MESH = pl.DeviceIdType.MESH
PEERS = ("gz", "gy")


def peer_device(peer):
    across = lax.axis_size("gy")
    return {"gz": lax.div(peer, across), "gy": lax.rem(peer, across)}


def exchange(peers, sent_ref, received_ref, send_sem, recv_sem):
    me = lax.axis_index(PEERS)

    def copy(step):
        peer = lax.rem(me + step, peers)
        return pltpu.make_async_remote_copy(
            src_ref=sent_ref.at[peer],
            dst_ref=received_ref.at[me],
            send_sem=send_sem.at[step],
            recv_sem=recv_sem.at[step],
            device_id=peer_device(peer),
            device_id_type=MESH,
        )

    return copy


def greet_peers(peers):
    me = lax.axis_index(PEERS)
    barrier = pltpu.get_barrier_semaphore()

    def greet(step, carry):
        pl.semaphore_signal(
            barrier, inc=1, device_id=peer_device(lax.rem(me + step, peers)), device_id_type=MESH
        )
        return carry

    lax.fori_loop(1, peers, greet, 0)
    return barrier


def route_part(peers, rows, target_ref, payload_ref, sent_ref, slot_ref, left_ref, right_ref):
    chunks = target_ref.shape[0]
    target = target_ref[...]
    bf16 = jnp.bfloat16
    upper = (iota((LANES, LANES), 0) < iota((LANES, LANES), 1)).astype(bf16)
    lower = (iota((chunks, chunks), 1) < iota((chunks, chunks), 0)).astype(bf16)
    ones = jnp.ones((LANES, LANES), bf16)

    def ranked(peer, rank):
        mask = target == peer
        onehot = mask.astype(jnp.float32).astype(bf16)
        within = lax.dot_general(onehot, upper, NN, preferred_element_type=jnp.float32)
        ahead = lax.dot_general(lower, onehot, NN, preferred_element_type=jnp.float32)
        before = lax.dot_general(ahead.astype(bf16), ones, NN, preferred_element_type=jnp.float32)
        return jnp.where(mask, within + before, rank)

    rank = lax.fori_loop(0, peers, ranked, jnp.zeros(target.shape, jnp.float32)).astype(jnp.int32)
    slot_ref[0] = jnp.where(target < 0, -1, target * rows + lax.div(rank, LANES))
    slot_ref[1] = lax.rem(rank, LANES)
    height = left_ref.shape[0] // 15

    def place(chunk, carry):
        at = pl.ds(pl.multiple_of(chunk * LANES, LANES), LANES)
        high_mask = iota((height, LANES), 0) == slot_ref[0, pl.ds(chunk, 1), :]
        low_mask = iota((LANES, LANES), 0) == slot_ref[1, pl.ds(chunk, 1), :]
        right_ref[:, at] = low_mask.astype(jnp.float32).astype(bf16)
        values = payload_ref[:, at]
        first = values.astype(bf16).astype(jnp.float32)
        rest = values - first
        second = rest.astype(bf16).astype(jnp.float32)
        third = rest - second
        piece = 0
        for row in range(6):
            for part in (first, second, third)[: 2 if row < 3 else 3]:
                left_ref[piece * height : (piece + 1) * height, at] = jnp.where(
                    high_mask, part[row : row + 1, :], 0.0
                ).astype(bf16)
                piece += 1
        return carry

    lax.fori_loop(0, chunks, place, 0)
    placed = lax.dot_general(
        left_ref[...], right_ref[...], NT, preferred_element_type=jnp.float32
    )
    piece = 0
    for row in range(6):
        count = 2 if row < 3 else 3
        total = placed[piece * height : (piece + 1) * height]
        for more in range(1, count):
            total = total + placed[(piece + more) * height : (piece + more + 1) * height]
        piece += count
        for peer in range(peers):
            sent_ref[peer, row * rows : (row + 1) * rows, :] = total[peer * rows : (peer + 1) * rows]


def stencil(position):
    base = jnp.floor(position)
    angle = (0.5 * math.pi) * (position - base)
    sine, cosine = jnp.sin(angle), jnp.cos(angle)
    weights = [0.25 - 0.25 * sine, 0.25 + 0.25 * cosine, 0.25 + 0.25 * sine, 0.25 - 0.25 * cosine]
    return base.astype(jnp.int32), weights


def node_weights(size, base, weights, row):
    step = iota((size, LANES), 0) - base[row : row + 1, :]
    result = jnp.zeros((size, LANES), jnp.float32)
    for index in range(4):
        result = jnp.where(step == index - 1, weights[index][row : row + 1, :], result)
    return result


def spread_part(sizes, rows, block, left_ref, right_ref, total_ref):
    size_x, size_y, size_z = sizes
    height = 3 * size_x * size_y
    base, weights = stencil(block[3 * rows : 6 * rows])
    for k in range(rows):
        at = slice(k * LANES, (k + 1) * LANES)
        along_x = node_weights(size_x, base, weights, k)
        along_y = node_weights(size_y, base, weights, rows + k)
        high, low = split_two(node_weights(size_z, base, weights, 2 * rows + k))
        right_ref[:size_z, at] = high
        right_ref[size_z:, at] = low
        for dimension in range(3):
            scaled = along_x * block[dimension * rows + k : dimension * rows + k + 1, :]
            for x in range(size_x):
                first = (dimension * size_x + x) * size_y
                high, low = split_two(along_y * scaled[x : x + 1, :])
                left_ref[first : first + size_y, at] = high
                left_ref[height + first : height + first + size_y, at] = low
    total_ref[...] += lax.dot_general(
        left_ref[...], right_ref[...], NT, preferred_element_type=jnp.float32
    )


def outward_kernel(
    peers, rows, sizes, target_ref, payload_ref, field_ref, slot_ref, position_ref,
    route_left, route_right, sent_ref, arrived_ref, left_ref, right_ref, total_ref,
    send_sem, recv_sem,
):
    me = lax.axis_index(PEERS)
    size_z = sizes[2]
    height = 3 * sizes[0] * sizes[1]
    barrier = greet_peers(peers)
    route_part(peers, rows, target_ref, payload_ref, sent_ref, slot_ref, route_left, route_right)
    pl.semaphore_wait(barrier, peers - 1)
    copy = exchange(peers, sent_ref, arrived_ref, send_sem, recv_sem)

    def send(step, carry):
        copy(step).start()
        return carry

    lax.fori_loop(1, peers, send, 0)
    total_ref[...] = jnp.zeros_like(total_ref)

    def add(source, block):
        position_ref[source] = block[3 * rows : 6 * rows]
        spread_part(sizes, rows, block, left_ref, right_ref, total_ref)

    add(me, sent_ref[me])

    def one(step, carry):
        copy(step).wait_recv()
        source = lax.rem(me + peers - step, peers)
        add(source, arrived_ref[source])
        return carry

    lax.fori_loop(1, peers, one, 0)
    field_ref[...] = (total_ref[height:, size_z:] + total_ref[height:, :size_z]) + (
        total_ref[:height, size_z:] + total_ref[:height, :size_z]
    )

    def finish(step, carry):
        copy(step).wait_send()
        return carry

    lax.fori_loop(1, peers, finish, 0)


def outward(target, payload, peers, rows, sizes):
    chunks = target.shape[0]
    slots_high = -(-peers * rows // 16) * 16
    height = 3 * sizes[0] * sizes[1]
    return pl.pallas_call(
        lambda *refs: outward_kernel(peers, rows, sizes, *refs),
        out_shape=(
            jax.ShapeDtypeStruct((height, sizes[2]), jnp.float32),
            jax.ShapeDtypeStruct((2, chunks, LANES), jnp.int32),
            jax.ShapeDtypeStruct((peers, 3 * rows, LANES), jnp.float32),
        ),
        in_specs=[pl.BlockSpec(memory_space=pltpu.VMEM)] * 2,
        out_specs=(pl.BlockSpec(memory_space=pltpu.VMEM),) * 3,
        scratch_shapes=[
            pltpu.VMEM((15 * slots_high, chunks * LANES), jnp.bfloat16),
            pltpu.VMEM((LANES, chunks * LANES), jnp.bfloat16),
            pltpu.VMEM((peers, 6 * rows, LANES), jnp.float32),
            pltpu.VMEM((peers, 6 * rows, LANES), jnp.float32),
            pltpu.VMEM((2 * height, rows * LANES), jnp.bfloat16),
            pltpu.VMEM((2 * sizes[2], rows * LANES), jnp.bfloat16),
            pltpu.VMEM((2 * height, 2 * sizes[2]), jnp.float32),
            pltpu.SemaphoreType.DMA((peers,)),
            pltpu.SemaphoreType.DMA((peers,)),
        ],
        compiler_params=pltpu.CompilerParams(
            vmem_limit_bytes=VMEM_LIMIT, collective_id=0, has_side_effects=True
        ),
        name="outward",
    )(target, payload)


def sample_part(sizes, rows, position, left_ref, right_ref, part_ref):
    size_x, size_y, size_z = sizes
    base, weights = stencil(position)
    for k in range(rows):
        at = slice(k * LANES, (k + 1) * LANES)
        high, low = split_two(node_weights(size_z, base, weights, 2 * rows + k))
        right_ref[:size_z, at] = high
        right_ref[size_z : 2 * size_z, at] = high
        right_ref[2 * size_z :, at] = low
    part_ref[...] = lax.dot_general(
        left_ref[...], right_ref[...], NN, preferred_element_type=jnp.float32
    )
    result = [[], [], []]
    for k in range(rows):
        at = slice(k * LANES, (k + 1) * LANES)
        along_x = node_weights(size_x, base, weights, k)
        along_y = node_weights(size_y, base, weights, rows + k)
        for dimension in range(3):
            total = jnp.zeros((size_y, LANES), jnp.float32)
            for x in range(size_x):
                first = (dimension * size_x + x) * size_y
                total = total + along_x[x : x + 1, :] * part_ref[first : first + size_y, at]
            result[dimension].append(jnp.sum(total * along_y, axis=0, keepdims=True))
    return jnp.concatenate(result[0] + result[1] + result[2], axis=0) / VELOCITY_UNIT


def collect_part(peers, rows, returned_ref, slot_ref, result_ref, table_ref, left_ref):
    height = left_ref.shape[0] // 3
    markers = result_ref.shape[1]
    table_ref[...] = jnp.zeros_like(table_ref)
    for row in range(3):
        for peer in range(peers):
            first = row * height + peer * rows
            table_ref[first : first + rows, :] = returned_ref[peer, row * rows : (row + 1) * rows, :]
    high, low = split_two(table_ref[...])
    left_ref[:, :LANES] = high
    left_ref[:, LANES:] = low

    def one(chunk):
        low_mask = iota((LANES, LANES), 0) == slot_ref[1, pl.ds(chunk, 1), :]
        onehot = low_mask.astype(jnp.float32).astype(jnp.bfloat16)
        found = lax.dot_general(
            left_ref[...],
            jnp.concatenate([onehot, onehot], axis=0),
            NN,
            preferred_element_type=jnp.float32,
        )
        high_mask = iota((height, LANES), 0) == slot_ref[0, pl.ds(chunk, 1), :]
        return jnp.concatenate(
            [
                jnp.sum(
                    jnp.where(high_mask, found[row * height : (row + 1) * height], 0.0),
                    axis=0,
                    keepdims=True,
                )
                for row in range(3)
            ],
            axis=0,
        )

    whole, rest = markers // LANES, markers % LANES

    def step(chunk, carry):
        result_ref[:, pl.ds(pl.multiple_of(chunk * LANES, LANES), LANES)] = one(chunk)
        return carry

    lax.fori_loop(0, whole, step, 0, unroll=4)
    if rest:
        result_ref[:, markers - rest :] = one(whole)[:, :rest]


def homeward_kernel(
    peers, rows, sizes, position_ref, velocity_ref, slot_ref, result_ref,
    sampled_ref, returned_ref, left_ref, right_ref, part_ref, table_ref, table_left,
    send_sem, recv_sem,
):
    me = lax.axis_index(PEERS)
    size_z = sizes[2]
    barrier = greet_peers(peers)
    high, low = split_two(velocity_ref[...])
    left_ref[:, :size_z] = high
    left_ref[:, size_z : 2 * size_z] = low
    left_ref[:, 2 * size_z :] = high
    pl.semaphore_wait(barrier, peers - 1)
    copy = exchange(peers, sampled_ref, returned_ref, send_sem, recv_sem)

    def one(step, carry):
        peer = lax.rem(me + step, peers)
        sampled_ref[peer] = sample_part(
            sizes, rows, position_ref[peer], left_ref, right_ref, part_ref
        )
        copy(step).start()
        return carry

    lax.fori_loop(1, peers, one, 0)
    returned_ref[me] = sample_part(sizes, rows, position_ref[me], left_ref, right_ref, part_ref)

    def finish(step, carry):
        copy(step).wait_recv()
        copy(step).wait_send()
        return carry

    lax.fori_loop(1, peers, finish, 0)
    collect_part(peers, rows, returned_ref, slot_ref, result_ref, table_ref, table_left)


def homeward(position, velocity, slots, markers, rows, sizes):
    peers = position.shape[0]
    slots_high = -(-peers * rows // 16) * 16
    height = 3 * sizes[0] * sizes[1]
    return pl.pallas_call(
        lambda *refs: homeward_kernel(peers, rows, sizes, *refs),
        out_shape=jax.ShapeDtypeStruct((3, markers), jnp.float32),
        in_specs=[pl.BlockSpec(memory_space=pltpu.VMEM)] * 3,
        out_specs=pl.BlockSpec(memory_space=pltpu.VMEM),
        scratch_shapes=[
            pltpu.VMEM((peers, 3 * rows, LANES), jnp.float32),
            pltpu.VMEM((peers, 3 * rows, LANES), jnp.float32),
            pltpu.VMEM((height, 3 * sizes[2]), jnp.bfloat16),
            pltpu.VMEM((3 * sizes[2], rows * LANES), jnp.bfloat16),
            pltpu.VMEM((height, rows * LANES), jnp.float32),
            pltpu.VMEM((3 * slots_high, LANES), jnp.float32),
            pltpu.VMEM((3 * slots_high, 2 * LANES), jnp.bfloat16),
            pltpu.SemaphoreType.DMA((peers,)),
            pltpu.SemaphoreType.DMA((peers,)),
        ],
        compiler_params=pltpu.CompilerParams(
            vmem_limit_bytes=VMEM_LIMIT, collective_id=1, has_side_effects=True
        ),
        name="homeward",
    )(position, velocity, slots)


def moving_rows(dimension):
    return [index for index in range(19) if int(LATTICE[index][dimension]) != 0]


def shift_along(field, padded, moving, dimension, length):
    pieces = [field[index] for index in range(19)]
    for slot_pos, index in enumerate(moving):
        first_cell = 1 - int(LATTICE[index][dimension])
        pieces[index] = lax.slice_in_dim(
            padded[slot_pos], first_cell, first_cell + length, axis=dimension
        )
    return jnp.stack(pieces)


def shards(populations, displacement, stiffness, base_node, offset, destination):
    size_x, size_y, size_z = (populations.shape[1], populations.shape[2], populations.shape[3])
    peer_count = lax.axis_size(("gz", "gy"))
    markers = displacement.shape[1]
    capacity = max(2, (2 * markers + peer_count - 1) // peer_count)
    rows = -(-capacity // LANES)
    chunks = -(-markers // LANES)
    spare = chunks * LANES - markers
    sizes = (size_x, size_y, size_z)
    forces = marker_forces(displacement, stiffness)
    position = base_node.astype(jnp.float32) + offset
    target = jnp.pad(destination[:, 0], (0, spare), constant_values=-1).reshape(chunks, LANES)
    payload = jnp.pad(jnp.concatenate([forces, position], axis=0), ((0, 0), (0, spare)))
    field, slots, marker_position = outward(target, payload, peer_count, rows, sizes)
    force_field = field.reshape(3, size_x, size_y, size_z)
    post = collide(populations, force_field)
    moving = moving_rows(0)
    padded = padded_2(jnp.stack([post[index] for index in moving]), (("gx", 1),), 1)
    post = shift_along(post, padded, moving, 0, size_x)
    moving = moving_rows(1)
    padded = padded_2(jnp.stack([post[index] for index in moving]), (("gy", 2),), 1)
    post = shift_along(post, padded, moving, 1, size_y)
    moving = moving_rows(2)
    padded = padded_2(jnp.stack([post[index] for index in moving]), (("gz", 3),), 1)
    new_populations = shift_along(post, padded, moving, 2, size_z)
    velocity = fluid_velocity(new_populations).reshape(3 * size_x * size_y, size_z)
    marker_velocity = homeward(marker_position, velocity, slots, markers, rows, sizes)
    return (new_populations, marker_velocity)


def solution(mesh):
    return jax.shard_map(
        shards,
        mesh=mesh,
        in_specs=(
            P(None, ("groups", "gx"), "gy", "gz"),
            P(None, ("groups", "gz", "gy", "gx")),
            P(("groups", "gz", "gy", "gx")),
            P(None, ("groups", "gz", "gy", "gx")),
            P(None, ("groups", "gz", "gy", "gx")),
            P(("groups", "gz", "gy", "gx"), None),
        ),
        out_specs=(P(None, ("groups", "gx"), "gy", "gz"), P(None, ("groups", "gz", "gy", "gx"))),
        check_vma=False,
    )
```

```python
import math

import jax
import jax.numpy as jnp
import numpy as np
from jax import lax
from jax.experimental import pallas as pl
from jax.experimental.pallas import tpu as pltpu
from jax.sharding import PartitionSpec as P

LATTICE = np.array(
    [
        [0, 0, 0],
        [1, 0, 0],
        [-1, 0, 0],
        [0, 1, 0],
        [0, -1, 0],
        [0, 0, 1],
        [0, 0, -1],
        [1, 1, 0],
        [-1, -1, 0],
        [1, -1, 0],
        [-1, 1, 0],
        [1, 0, 1],
        [-1, 0, -1],
        [1, 0, -1],
        [-1, 0, 1],
        [0, 1, 1],
        [0, -1, -1],
        [0, 1, -1],
        [0, -1, 1],
    ]
)
WEIGHTS = [1.0 / 3.0] + [1.0 / 18.0] * 6 + [1.0 / 36.0] * 12
RELAXATION = 0.8
VELOCITY_UNIT = 0.01
MESH = pl.DeviceIdType.MESH


def marker_forces(displacement, stiffness):
    grouped = displacement.reshape(3, stiffness.shape[0], -1)
    centred = grouped - jnp.mean(grouped, axis=2, keepdims=True)
    return (stiffness[None, :, None] * centred).reshape(3, -1)


def momentum_sum(populations, dimension):
    total = jnp.zeros_like(populations[0])
    for index in range(19):
        step_sign = int(LATTICE[index][dimension])
        if step_sign != 0:
            total = total + step_sign * populations[index]
    return total


def collide(populations, force_field):
    density = sum(populations[1:], populations[0])
    velocity = [
        (momentum_sum(populations, dimension) + 0.5 * force_field[dimension]) / density
        for dimension in range(3)
    ]
    speed_squared = (
        velocity[0] * velocity[0] + velocity[1] * velocity[1] + velocity[2] * velocity[2]
    )
    factor = 1.0 - 0.5 / RELAXATION
    result = []
    for index in range(19):
        lattice_row = [int(value) for value in LATTICE[index]]
        along = jnp.zeros_like(density)
        for dimension in range(3):
            if lattice_row[dimension] != 0:
                along = along + lattice_row[dimension] * velocity[dimension]
        equilibrium = (
            WEIGHTS[index]
            * density
            * (1.0 + 3.0 * along + 4.5 * along * along - 1.5 * speed_squared)
        )
        source = jnp.zeros_like(density)
        for dimension in range(3):
            source = (
                source
                + (
                    3.0 * (lattice_row[dimension] - velocity[dimension])
                    + 9.0 * along * lattice_row[dimension]
                )
                * force_field[dimension]
            )
        result.append(
            populations[index]
            - (populations[index] - equilibrium) / RELAXATION
            + factor * WEIGHTS[index] * source
        )
    return result


def directions(dimension, sign):
    return [index for index in range(19) if int(LATTICE[index][dimension]) == sign]


AXES = ("gx", "gy", "gz")
FACES = [(dimension, sign) for dimension in range(3) for sign in (1, -1)]


def neighbour(dimension, sign):
    size = lax.axis_size(AXES[dimension])
    return {AXES[dimension]: lax.rem(lax.axis_index(AXES[dimension]) + size + sign, size)}


def fluid_kernel(
    populations_ref, field_ref, result_ref, velocity_ref,
    out_x, out_y, out_z, in_x, in_y, in_z, send_sem, recv_sem,
):
    size_x, size_y, size_z = populations_ref.shape[1:]
    barrier = pltpu.get_barrier_semaphore()
    for face in FACES:
        pl.semaphore_signal(barrier, inc=1, device_id=neighbour(*face), device_id_type=MESH)

    def collided(x):
        return collide(
            [populations_ref[index, x] for index in range(19)],
            [field_ref[dimension, x] for dimension in range(3)],
        )

    def copy(face, source, target):
        dimension, sign = FACES[face]
        return pltpu.make_async_remote_copy(
            src_ref=source.at[face % 2],
            dst_ref=target.at[face % 2],
            send_sem=send_sem.at[face],
            recv_sem=recv_sem.at[face],
            device_id=neighbour(dimension, sign),
            device_id_type=MESH,
        )

    first, last = collided(0), collided(size_x - 1)
    for slot, index in enumerate(directions(0, 1)):
        out_x[0, slot] = last[index]
        result_ref[index, 1] = first[index]
    for slot, index in enumerate(directions(0, -1)):
        out_x[1, slot] = first[index]
        result_ref[index, size_x - 2] = last[index]
    for index in directions(0, 0):
        result_ref[index, 0] = first[index]
        result_ref[index, size_x - 1] = last[index]
    pl.semaphore_wait(barrier, len(FACES))
    copies = [copy(face, out_x, in_x) for face in (0, 1)]
    for one in copies:
        one.start()

    def inner(x, carry):
        post = collided(x)
        for index in range(19):
            result_ref[index, x + int(LATTICE[index][0])] = post[index]
        return carry

    lax.fori_loop(1, size_x - 1, inner, 0)
    for one in copies:
        one.wait_recv()
    for slot, index in enumerate(directions(0, 1)):
        result_ref[index, 0] = in_x[0, slot]
    for slot, index in enumerate(directions(0, -1)):
        result_ref[index, size_x - 1] = in_x[1, slot]

    for side, sign in enumerate((1, -1)):
        edge = size_y - 1 if sign == 1 else 0
        for slot, index in enumerate(directions(1, sign)):
            out_y[side, slot] = jnp.concatenate(
                [result_ref[index, x, edge : edge + 1, :] for x in range(size_x)], axis=0
            )
    copies_y = [copy(face, out_y, in_y) for face in (2, 3)]
    for one in copies_y:
        one.start()
    for one in copies_y:
        one.wait_recv()
    for side, sign in enumerate((1, -1)):
        for slot, index in enumerate(directions(1, sign)):
            for x in range(size_x):
                plane = result_ref[index, x]
                row = in_y[side, slot, x : x + 1, :]
                result_ref[index, x] = jnp.concatenate(
                    [row, plane[: size_y - 1]] if sign == 1 else [plane[1:], row], axis=0
                )

    lane = iota((size_y, size_z), 1)
    for side, sign in enumerate((1, -1)):
        edge = size_z - 1 if sign == 1 else 0
        packed = jnp.zeros((size_y, size_z), jnp.float32)
        for slot, index in enumerate(directions(2, sign)):
            for x in range(size_x):
                packed = jnp.where(
                    lane == slot * size_x + x, result_ref[index, x, :, edge : edge + 1], packed
                )
        out_z[side] = packed
    copies_z = [copy(face, out_z, in_z) for face in (4, 5)]
    for one in copies_z:
        one.start()
    for one in copies_z:
        one.wait_recv()
    for side, sign in enumerate((1, -1)):
        edge = 0 if sign == 1 else size_z - 1
        arrived = in_z[side]
        for slot, index in enumerate(directions(2, sign)):
            for x in range(size_x):
                at = slot * size_x + x
                turned = pltpu.roll(result_ref[index, x], 1 if sign == 1 else size_z - 1, axis=1)
                result_ref[index, x] = jnp.where(lane == edge, arrived[:, at : at + 1], turned)

    def speed(x, carry):
        planes = [result_ref[index, x] for index in range(19)]
        density = sum(planes[1:], planes[0])
        for dimension in range(3):
            velocity_ref[dimension, x] = momentum_sum(planes, dimension) / density
        return carry

    lax.fori_loop(0, size_x, speed, 0)
    for one in copies + copies_y + copies_z:
        one.wait_send()


def fluid(populations, force_field):
    size_x, size_y, size_z = populations.shape[1:]
    moving = len(directions(0, 1))
    assert moving * size_x <= size_z
    faces = [
        (2, moving, size_y, size_z),
        (2, moving, size_x, size_z),
        (2, size_y, size_z),
    ]
    return pl.pallas_call(
        fluid_kernel,
        out_shape=(
            jax.ShapeDtypeStruct(populations.shape, jnp.float32),
            jax.ShapeDtypeStruct((3, size_x, size_y, size_z), jnp.float32),
        ),
        in_specs=[pl.BlockSpec(memory_space=pltpu.VMEM)] * 2,
        out_specs=(pl.BlockSpec(memory_space=pltpu.VMEM),) * 2,
        scratch_shapes=[pltpu.VMEM(shape, jnp.float32) for shape in faces + faces]
        + [pltpu.SemaphoreType.DMA((len(FACES),)), pltpu.SemaphoreType.DMA((len(FACES),))],
        compiler_params=pltpu.CompilerParams(
            vmem_limit_bytes=VMEM_LIMIT, collective_id=2, has_side_effects=True
        ),
        name="fluid",
    )(populations, force_field)


LANES = 128
VMEM_LIMIT = 48 * 1024 * 1024
NT = (((1,), (1,)), ((), ()))
NN = (((1,), (0,)), ((), ()))


def iota(shape, dimension):
    return lax.broadcasted_iota(jnp.int32, shape, dimension)


def split_two(value):
    high = value.astype(jnp.bfloat16)
    return high, (value - high.astype(jnp.float32)).astype(jnp.bfloat16)


PEERS = ("gz", "gy")


def peer_device(peer):
    across = lax.axis_size("gy")
    return {"gz": lax.div(peer, across), "gy": lax.rem(peer, across)}


def exchange(peers, sent_ref, received_ref, send_sem, recv_sem):
    me = lax.axis_index(PEERS)

    def copy(step):
        peer = lax.rem(me + step, peers)
        return pltpu.make_async_remote_copy(
            src_ref=sent_ref.at[peer],
            dst_ref=received_ref.at[me],
            send_sem=send_sem.at[step],
            recv_sem=recv_sem.at[step],
            device_id=peer_device(peer),
            device_id_type=MESH,
        )

    return copy


def greet_peers(peers):
    me = lax.axis_index(PEERS)
    barrier = pltpu.get_barrier_semaphore()

    def greet(step, carry):
        pl.semaphore_signal(
            barrier, inc=1, device_id=peer_device(lax.rem(me + step, peers)), device_id_type=MESH
        )
        return carry

    lax.fori_loop(1, peers, greet, 0)
    return barrier


def route_part(peers, rows, target_ref, payload_ref, sent_ref, slot_ref, left_ref, right_ref):
    chunks = target_ref.shape[0]
    target = target_ref[...]
    bf16 = jnp.bfloat16
    upper = (iota((LANES, LANES), 0) < iota((LANES, LANES), 1)).astype(bf16)
    lower = (iota((chunks, chunks), 1) < iota((chunks, chunks), 0)).astype(bf16)
    ones = jnp.ones((LANES, LANES), bf16)

    def ranked(peer, rank):
        mask = target == peer
        onehot = mask.astype(jnp.float32).astype(bf16)
        within = lax.dot_general(onehot, upper, NN, preferred_element_type=jnp.float32)
        ahead = lax.dot_general(lower, onehot, NN, preferred_element_type=jnp.float32)
        before = lax.dot_general(ahead.astype(bf16), ones, NN, preferred_element_type=jnp.float32)
        return jnp.where(mask, within + before, rank)

    rank = lax.fori_loop(0, peers, ranked, jnp.zeros(target.shape, jnp.float32)).astype(jnp.int32)
    slot_ref[0] = jnp.where(target < 0, -1, target * rows + lax.div(rank, LANES))
    slot_ref[1] = lax.rem(rank, LANES)
    height = left_ref.shape[0] // 15

    def place(chunk, carry):
        at = pl.ds(pl.multiple_of(chunk * LANES, LANES), LANES)
        high_mask = iota((height, LANES), 0) == slot_ref[0, pl.ds(chunk, 1), :]
        low_mask = iota((LANES, LANES), 0) == slot_ref[1, pl.ds(chunk, 1), :]
        right_ref[:, at] = low_mask.astype(jnp.float32).astype(bf16)
        values = payload_ref[:, at]
        first = values.astype(bf16).astype(jnp.float32)
        rest = values - first
        second = rest.astype(bf16).astype(jnp.float32)
        third = rest - second
        piece = 0
        for row in range(6):
            for part in (first, second, third)[: 2 if row < 3 else 3]:
                left_ref[piece * height : (piece + 1) * height, at] = jnp.where(
                    high_mask, part[row : row + 1, :], 0.0
                ).astype(bf16)
                piece += 1
        return carry

    lax.fori_loop(0, chunks, place, 0)
    placed = lax.dot_general(
        left_ref[...], right_ref[...], NT, preferred_element_type=jnp.float32
    )
    piece = 0
    for row in range(6):
        count = 2 if row < 3 else 3
        total = placed[piece * height : (piece + 1) * height]
        for more in range(1, count):
            total = total + placed[(piece + more) * height : (piece + more + 1) * height]
        piece += count
        for peer in range(peers):
            sent_ref[peer, row * rows : (row + 1) * rows, :] = total[peer * rows : (peer + 1) * rows]


def stencil(position):
    base = jnp.floor(position)
    angle = (0.5 * math.pi) * (position - base)
    sine, cosine = jnp.sin(angle), jnp.cos(angle)
    weights = [0.25 - 0.25 * sine, 0.25 + 0.25 * cosine, 0.25 + 0.25 * sine, 0.25 - 0.25 * cosine]
    return base.astype(jnp.int32), weights


def node_weights(size, base, weights, row):
    step = iota((size, LANES), 0) - base[row : row + 1, :]
    result = jnp.zeros((size, LANES), jnp.float32)
    for index in range(4):
        result = jnp.where(step == index - 1, weights[index][row : row + 1, :], result)
    return result


def spread_part(sizes, rows, block, left_ref, right_ref, total_ref):
    size_x, size_y, size_z = sizes
    height = 3 * size_x * size_y
    base, weights = stencil(block[3 * rows : 6 * rows])
    for k in range(rows):
        at = slice(k * LANES, (k + 1) * LANES)
        along_x = node_weights(size_x, base, weights, k)
        along_y = node_weights(size_y, base, weights, rows + k)
        high, low = split_two(node_weights(size_z, base, weights, 2 * rows + k))
        right_ref[:size_z, at] = high
        right_ref[size_z:, at] = low
        for dimension in range(3):
            scaled = along_x * block[dimension * rows + k : dimension * rows + k + 1, :]
            for x in range(size_x):
                first = (dimension * size_x + x) * size_y
                high, low = split_two(along_y * scaled[x : x + 1, :])
                left_ref[first : first + size_y, at] = high
                left_ref[height + first : height + first + size_y, at] = low
    total_ref[...] += lax.dot_general(
        left_ref[...], right_ref[...], NT, preferred_element_type=jnp.float32
    )


def outward_kernel(
    peers, rows, sizes, target_ref, payload_ref, field_ref, slot_ref, position_ref,
    route_left, route_right, sent_ref, arrived_ref, left_ref, right_ref, total_ref,
    send_sem, recv_sem,
):
    me = lax.axis_index(PEERS)
    size_z = sizes[2]
    height = 3 * sizes[0] * sizes[1]
    barrier = greet_peers(peers)
    route_part(peers, rows, target_ref, payload_ref, sent_ref, slot_ref, route_left, route_right)
    pl.semaphore_wait(barrier, peers - 1)
    copy = exchange(peers, sent_ref, arrived_ref, send_sem, recv_sem)

    def send(step, carry):
        copy(step).start()
        return carry

    lax.fori_loop(1, peers, send, 0)
    total_ref[...] = jnp.zeros_like(total_ref)

    def add(source, block):
        position_ref[source] = block[3 * rows : 6 * rows]
        spread_part(sizes, rows, block, left_ref, right_ref, total_ref)

    add(me, sent_ref[me])

    def one(step, carry):
        copy(step).wait_recv()
        source = lax.rem(me + peers - step, peers)
        add(source, arrived_ref[source])
        return carry

    lax.fori_loop(1, peers, one, 0)
    field_ref[...] = (total_ref[height:, size_z:] + total_ref[height:, :size_z]) + (
        total_ref[:height, size_z:] + total_ref[:height, :size_z]
    )

    def finish(step, carry):
        copy(step).wait_send()
        return carry

    lax.fori_loop(1, peers, finish, 0)


def outward(target, payload, peers, rows, sizes):
    chunks = target.shape[0]
    slots_high = -(-peers * rows // 16) * 16
    height = 3 * sizes[0] * sizes[1]
    return pl.pallas_call(
        lambda *refs: outward_kernel(peers, rows, sizes, *refs),
        out_shape=(
            jax.ShapeDtypeStruct((height, sizes[2]), jnp.float32),
            jax.ShapeDtypeStruct((2, chunks, LANES), jnp.int32),
            jax.ShapeDtypeStruct((peers, 3 * rows, LANES), jnp.float32),
        ),
        in_specs=[pl.BlockSpec(memory_space=pltpu.VMEM)] * 2,
        out_specs=(pl.BlockSpec(memory_space=pltpu.VMEM),) * 3,
        scratch_shapes=[
            pltpu.VMEM((15 * slots_high, chunks * LANES), jnp.bfloat16),
            pltpu.VMEM((LANES, chunks * LANES), jnp.bfloat16),
            pltpu.VMEM((peers, 6 * rows, LANES), jnp.float32),
            pltpu.VMEM((peers, 6 * rows, LANES), jnp.float32),
            pltpu.VMEM((2 * height, rows * LANES), jnp.bfloat16),
            pltpu.VMEM((2 * sizes[2], rows * LANES), jnp.bfloat16),
            pltpu.VMEM((2 * height, 2 * sizes[2]), jnp.float32),
            pltpu.SemaphoreType.DMA((peers,)),
            pltpu.SemaphoreType.DMA((peers,)),
        ],
        compiler_params=pltpu.CompilerParams(
            vmem_limit_bytes=VMEM_LIMIT, collective_id=0, has_side_effects=True
        ),
        name="outward",
    )(target, payload)


def sample_part(sizes, rows, position, left_ref, right_ref, part_ref):
    size_x, size_y, size_z = sizes
    base, weights = stencil(position)
    for k in range(rows):
        at = slice(k * LANES, (k + 1) * LANES)
        high, low = split_two(node_weights(size_z, base, weights, 2 * rows + k))
        right_ref[:size_z, at] = high
        right_ref[size_z : 2 * size_z, at] = high
        right_ref[2 * size_z :, at] = low
    part_ref[...] = lax.dot_general(
        left_ref[...], right_ref[...], NN, preferred_element_type=jnp.float32
    )
    result = [[], [], []]
    for k in range(rows):
        at = slice(k * LANES, (k + 1) * LANES)
        along_x = node_weights(size_x, base, weights, k)
        along_y = node_weights(size_y, base, weights, rows + k)
        for dimension in range(3):
            total = jnp.zeros((size_y, LANES), jnp.float32)
            for x in range(size_x):
                first = (dimension * size_x + x) * size_y
                total = total + along_x[x : x + 1, :] * part_ref[first : first + size_y, at]
            result[dimension].append(jnp.sum(total * along_y, axis=0, keepdims=True))
    return jnp.concatenate(result[0] + result[1] + result[2], axis=0) / VELOCITY_UNIT


def collect_part(peers, rows, returned_ref, slot_ref, result_ref, table_ref, left_ref):
    height = left_ref.shape[0] // 3
    markers = result_ref.shape[1]
    table_ref[...] = jnp.zeros_like(table_ref)
    for row in range(3):
        for peer in range(peers):
            first = row * height + peer * rows
            table_ref[first : first + rows, :] = returned_ref[peer, row * rows : (row + 1) * rows, :]
    high, low = split_two(table_ref[...])
    left_ref[:, :LANES] = high
    left_ref[:, LANES:] = low

    def one(chunk):
        low_mask = iota((LANES, LANES), 0) == slot_ref[1, pl.ds(chunk, 1), :]
        onehot = low_mask.astype(jnp.float32).astype(jnp.bfloat16)
        found = lax.dot_general(
            left_ref[...],
            jnp.concatenate([onehot, onehot], axis=0),
            NN,
            preferred_element_type=jnp.float32,
        )
        high_mask = iota((height, LANES), 0) == slot_ref[0, pl.ds(chunk, 1), :]
        return jnp.concatenate(
            [
                jnp.sum(
                    jnp.where(high_mask, found[row * height : (row + 1) * height], 0.0),
                    axis=0,
                    keepdims=True,
                )
                for row in range(3)
            ],
            axis=0,
        )

    whole, rest = markers // LANES, markers % LANES

    def step(chunk, carry):
        result_ref[:, pl.ds(pl.multiple_of(chunk * LANES, LANES), LANES)] = one(chunk)
        return carry

    lax.fori_loop(0, whole, step, 0, unroll=4)
    if rest:
        result_ref[:, markers - rest :] = one(whole)[:, :rest]


def homeward_kernel(
    peers, rows, sizes, position_ref, velocity_ref, slot_ref, result_ref,
    sampled_ref, returned_ref, left_ref, right_ref, part_ref, table_ref, table_left,
    send_sem, recv_sem,
):
    me = lax.axis_index(PEERS)
    size_z = sizes[2]
    barrier = greet_peers(peers)
    high, low = split_two(velocity_ref[...])
    left_ref[:, :size_z] = high
    left_ref[:, size_z : 2 * size_z] = low
    left_ref[:, 2 * size_z :] = high
    pl.semaphore_wait(barrier, peers - 1)
    copy = exchange(peers, sampled_ref, returned_ref, send_sem, recv_sem)

    def one(step, carry):
        peer = lax.rem(me + step, peers)
        sampled_ref[peer] = sample_part(
            sizes, rows, position_ref[peer], left_ref, right_ref, part_ref
        )
        copy(step).start()
        return carry

    lax.fori_loop(1, peers, one, 0)
    returned_ref[me] = sample_part(sizes, rows, position_ref[me], left_ref, right_ref, part_ref)

    def finish(step, carry):
        copy(step).wait_recv()
        copy(step).wait_send()
        return carry

    lax.fori_loop(1, peers, finish, 0)
    collect_part(peers, rows, returned_ref, slot_ref, result_ref, table_ref, table_left)


def homeward(position, velocity, slots, markers, rows, sizes):
    peers = position.shape[0]
    slots_high = -(-peers * rows // 16) * 16
    height = 3 * sizes[0] * sizes[1]
    return pl.pallas_call(
        lambda *refs: homeward_kernel(peers, rows, sizes, *refs),
        out_shape=jax.ShapeDtypeStruct((3, markers), jnp.float32),
        in_specs=[pl.BlockSpec(memory_space=pltpu.VMEM)] * 3,
        out_specs=pl.BlockSpec(memory_space=pltpu.VMEM),
        scratch_shapes=[
            pltpu.VMEM((peers, 3 * rows, LANES), jnp.float32),
            pltpu.VMEM((peers, 3 * rows, LANES), jnp.float32),
            pltpu.VMEM((height, 3 * sizes[2]), jnp.bfloat16),
            pltpu.VMEM((3 * sizes[2], rows * LANES), jnp.bfloat16),
            pltpu.VMEM((height, rows * LANES), jnp.float32),
            pltpu.VMEM((3 * slots_high, LANES), jnp.float32),
            pltpu.VMEM((3 * slots_high, 2 * LANES), jnp.bfloat16),
            pltpu.SemaphoreType.DMA((peers,)),
            pltpu.SemaphoreType.DMA((peers,)),
        ],
        compiler_params=pltpu.CompilerParams(
            vmem_limit_bytes=VMEM_LIMIT, collective_id=1, has_side_effects=True
        ),
        name="homeward",
    )(position, velocity, slots)


def shards(populations, displacement, stiffness, base_node, offset, destination):
    size_x, size_y, size_z = (populations.shape[1], populations.shape[2], populations.shape[3])
    peer_count = lax.axis_size(("gz", "gy"))
    markers = displacement.shape[1]
    capacity = max(2, (2 * markers + peer_count - 1) // peer_count)
    rows = -(-capacity // LANES)
    chunks = -(-markers // LANES)
    spare = chunks * LANES - markers
    sizes = (size_x, size_y, size_z)
    forces = marker_forces(displacement, stiffness)
    position = base_node.astype(jnp.float32) + offset
    target = jnp.pad(destination[:, 0], (0, spare), constant_values=-1).reshape(chunks, LANES)
    payload = jnp.pad(jnp.concatenate([forces, position], axis=0), ((0, 0), (0, spare)))
    field, slots, marker_position = outward(target, payload, peer_count, rows, sizes)
    force_field = field.reshape(3, size_x, size_y, size_z)
    new_populations, velocity = fluid(populations, force_field)
    velocity = velocity.reshape(3 * size_x * size_y, size_z)
    marker_velocity = homeward(marker_position, velocity, slots, markers, rows, sizes)
    return (new_populations, marker_velocity)


def solution(mesh):
    return jax.shard_map(
        shards,
        mesh=mesh,
        in_specs=(
            P(None, ("groups", "gx"), "gy", "gz"),
            P(None, ("groups", "gz", "gy", "gx")),
            P(("groups", "gz", "gy", "gx")),
            P(None, ("groups", "gz", "gy", "gx")),
            P(None, ("groups", "gz", "gy", "gx")),
            P(("groups", "gz", "gy", "gx"), None),
        ),
        out_specs=(P(None, ("groups", "gx"), "gy", "gz"), P(None, ("groups", "gz", "gy", "gx"))),
        check_vma=False,
    )
```

```python
import math

import jax
import jax.numpy as jnp
import numpy as np
from jax import lax
from jax.experimental import pallas as pl
from jax.experimental.pallas import tpu as pltpu
from jax.sharding import PartitionSpec as P

LATTICE = np.array(
    [
        [0, 0, 0],
        [1, 0, 0],
        [-1, 0, 0],
        [0, 1, 0],
        [0, -1, 0],
        [0, 0, 1],
        [0, 0, -1],
        [1, 1, 0],
        [-1, -1, 0],
        [1, -1, 0],
        [-1, 1, 0],
        [1, 0, 1],
        [-1, 0, -1],
        [1, 0, -1],
        [-1, 0, 1],
        [0, 1, 1],
        [0, -1, -1],
        [0, 1, -1],
        [0, -1, 1],
    ]
)
WEIGHTS = [1.0 / 3.0] + [1.0 / 18.0] * 6 + [1.0 / 36.0] * 12
RELAXATION = 0.8
VELOCITY_UNIT = 0.01
MESH = pl.DeviceIdType.MESH


def marker_forces(displacement, stiffness):
    grouped = displacement.reshape(3, stiffness.shape[0], -1)
    centred = grouped - jnp.mean(grouped, axis=2, keepdims=True)
    return (stiffness[None, :, None] * centred).reshape(3, -1)


def momentum_sum(populations, dimension):
    total = jnp.zeros_like(populations[0])
    for index in range(19):
        step_sign = int(LATTICE[index][dimension])
        if step_sign != 0:
            total = total + step_sign * populations[index]
    return total


def collide(populations, force_field):
    density = sum(populations[1:], populations[0])
    velocity = [
        (momentum_sum(populations, dimension) + 0.5 * force_field[dimension]) / density
        for dimension in range(3)
    ]
    speed_squared = (
        velocity[0] * velocity[0] + velocity[1] * velocity[1] + velocity[2] * velocity[2]
    )
    factor = 1.0 - 0.5 / RELAXATION
    result = []
    for index in range(19):
        lattice_row = [int(value) for value in LATTICE[index]]
        along = jnp.zeros_like(density)
        for dimension in range(3):
            if lattice_row[dimension] != 0:
                along = along + lattice_row[dimension] * velocity[dimension]
        equilibrium = (
            WEIGHTS[index]
            * density
            * (1.0 + 3.0 * along + 4.5 * along * along - 1.5 * speed_squared)
        )
        source = jnp.zeros_like(density)
        for dimension in range(3):
            source = (
                source
                + (
                    3.0 * (lattice_row[dimension] - velocity[dimension])
                    + 9.0 * along * lattice_row[dimension]
                )
                * force_field[dimension]
            )
        result.append(
            populations[index]
            - (populations[index] - equilibrium) / RELAXATION
            + factor * WEIGHTS[index] * source
        )
    return result


def directions(dimension, sign):
    return [index for index in range(19) if int(LATTICE[index][dimension]) == sign]


AXES = ("gx", "gy", "gz")
FACES = [(dimension, sign) for dimension in range(3) for sign in (1, -1)]


def neighbour(dimension, sign):
    size = lax.axis_size(AXES[dimension])
    return {AXES[dimension]: lax.rem(lax.axis_index(AXES[dimension]) + size + sign, size)}


def fluid_kernel(
    populations_ref, field_ref, result_ref, velocity_ref,
    out_x, out_y, out_z, in_x, in_y, in_z, send_sem, recv_sem,
):
    size_x, size_y, size_z = populations_ref.shape[1:]
    barrier = pltpu.get_barrier_semaphore()
    for face in FACES:
        pl.semaphore_signal(barrier, inc=1, device_id=neighbour(*face), device_id_type=MESH)

    def collided(x):
        return collide(
            [populations_ref[index, x] for index in range(19)],
            [field_ref[dimension, x] for dimension in range(3)],
        )

    def copy(face, source, target):
        dimension, sign = FACES[face]
        return pltpu.make_async_remote_copy(
            src_ref=source.at[face % 2],
            dst_ref=target.at[face % 2],
            send_sem=send_sem.at[face],
            recv_sem=recv_sem.at[face],
            device_id=neighbour(dimension, sign),
            device_id_type=MESH,
        )

    first, last = collided(0), collided(size_x - 1)
    for slot, index in enumerate(directions(0, 1)):
        out_x[0, slot] = last[index]
        result_ref[index, 1] = first[index]
    for slot, index in enumerate(directions(0, -1)):
        out_x[1, slot] = first[index]
        result_ref[index, size_x - 2] = last[index]
    for index in directions(0, 0):
        result_ref[index, 0] = first[index]
        result_ref[index, size_x - 1] = last[index]
    pl.semaphore_wait(barrier, len(FACES))
    copies = [copy(face, out_x, in_x) for face in (0, 1)]
    for one in copies:
        one.start()

    def inner(x, carry):
        post = collided(x)
        for index in range(19):
            result_ref[index, x + int(LATTICE[index][0])] = post[index]
        return carry

    lax.fori_loop(1, size_x - 1, inner, 0)
    for one in copies:
        one.wait_recv()
    for slot, index in enumerate(directions(0, 1)):
        result_ref[index, 0] = in_x[0, slot]
    for slot, index in enumerate(directions(0, -1)):
        result_ref[index, size_x - 1] = in_x[1, slot]

    for side, sign in enumerate((1, -1)):
        edge = size_y - 1 if sign == 1 else 0
        for slot, index in enumerate(directions(1, sign)):
            out_y[side, slot] = jnp.concatenate(
                [result_ref[index, x, edge : edge + 1, :] for x in range(size_x)], axis=0
            )
    copies_y = [copy(face, out_y, in_y) for face in (2, 3)]
    for one in copies_y:
        one.start()
    for one in copies_y:
        one.wait_recv()
    for side, sign in enumerate((1, -1)):
        for slot, index in enumerate(directions(1, sign)):
            for x in range(size_x):
                plane = result_ref[index, x]
                row = in_y[side, slot, x : x + 1, :]
                result_ref[index, x] = jnp.concatenate(
                    [row, plane[: size_y - 1]] if sign == 1 else [plane[1:], row], axis=0
                )

    lane = iota((size_y, size_z), 1)
    for side, sign in enumerate((1, -1)):
        edge = size_z - 1 if sign == 1 else 0
        packed = jnp.zeros((size_y, size_z), jnp.float32)
        for slot, index in enumerate(directions(2, sign)):
            for x in range(size_x):
                packed = jnp.where(
                    lane == slot * size_x + x, result_ref[index, x, :, edge : edge + 1], packed
                )
        out_z[side] = packed
    copies_z = [copy(face, out_z, in_z) for face in (4, 5)]
    for one in copies_z:
        one.start()
    for one in copies_z:
        one.wait_recv()
    for side, sign in enumerate((1, -1)):
        edge = 0 if sign == 1 else size_z - 1
        arrived = in_z[side]
        for slot, index in enumerate(directions(2, sign)):
            for x in range(size_x):
                at = slot * size_x + x
                turned = pltpu.roll(result_ref[index, x], 1 if sign == 1 else size_z - 1, axis=1)
                result_ref[index, x] = jnp.where(lane == edge, arrived[:, at : at + 1], turned)

    def speed(x, carry):
        planes = [result_ref[index, x] for index in range(19)]
        density = sum(planes[1:], planes[0])
        for dimension in range(3):
            velocity_ref[dimension, x] = momentum_sum(planes, dimension) / density
        return carry

    lax.fori_loop(0, size_x, speed, 0)
    for one in copies + copies_y + copies_z:
        one.wait_send()


def fluid(populations, force_field):
    size_x, size_y, size_z = populations.shape[1:]
    moving = len(directions(0, 1))
    assert moving * size_x <= size_z
    faces = [
        (2, moving, size_y, size_z),
        (2, moving, size_x, size_z),
        (2, size_y, size_z),
    ]
    return pl.pallas_call(
        fluid_kernel,
        out_shape=(
            jax.ShapeDtypeStruct(populations.shape, jnp.float32),
            jax.ShapeDtypeStruct((3, size_x, size_y, size_z), jnp.float32),
        ),
        in_specs=[pl.BlockSpec(memory_space=pltpu.VMEM)] * 2,
        out_specs=(pl.BlockSpec(memory_space=pltpu.VMEM),) * 2,
        scratch_shapes=[pltpu.VMEM(shape, jnp.float32) for shape in faces + faces]
        + [pltpu.SemaphoreType.DMA((len(FACES),)), pltpu.SemaphoreType.DMA((len(FACES),))],
        compiler_params=pltpu.CompilerParams(
            vmem_limit_bytes=VMEM_LIMIT, collective_id=2, has_side_effects=True
        ),
        name="fluid",
    )(populations, force_field)


LANES = 128
VMEM_LIMIT = 48 * 1024 * 1024
NT = (((1,), (1,)), ((), ()))
NN = (((1,), (0,)), ((), ()))


def iota(shape, dimension):
    return lax.broadcasted_iota(jnp.int32, shape, dimension)


def split_two(value):
    high = value.astype(jnp.bfloat16)
    return high, (value - high.astype(jnp.float32)).astype(jnp.bfloat16)


PEERS = ("gz", "gy")


def peer_device(peer):
    across = lax.axis_size("gy")
    return {"gz": lax.div(peer, across), "gy": lax.rem(peer, across)}


def exchange(peers, sent_ref, received_ref, send_sem, recv_sem):
    me = lax.axis_index(PEERS)

    def copy(step):
        peer = lax.rem(me + step, peers)
        return pltpu.make_async_remote_copy(
            src_ref=sent_ref.at[peer],
            dst_ref=received_ref.at[me],
            send_sem=send_sem.at[step],
            recv_sem=recv_sem.at[step],
            device_id=peer_device(peer),
            device_id_type=MESH,
        )

    return copy


def greet_peers(peers):
    me = lax.axis_index(PEERS)
    barrier = pltpu.get_barrier_semaphore()

    def greet(step, carry):
        pl.semaphore_signal(
            barrier, inc=1, device_id=peer_device(lax.rem(me + step, peers)), device_id_type=MESH
        )
        return carry

    lax.fori_loop(1, peers, greet, 0)
    return barrier


def route_part(peers, rows, target_ref, payload_ref, sent_ref, slot_ref, left_ref, right_ref):
    chunks = target_ref.shape[0]
    target = target_ref[...]
    bf16 = jnp.bfloat16
    upper = (iota((LANES, LANES), 0) < iota((LANES, LANES), 1)).astype(bf16)
    lower = (iota((chunks, chunks), 1) < iota((chunks, chunks), 0)).astype(bf16)
    ones = jnp.ones((LANES, LANES), bf16)

    def ranked(peer, rank):
        mask = target == peer
        onehot = mask.astype(jnp.float32).astype(bf16)
        within = lax.dot_general(onehot, upper, NN, preferred_element_type=jnp.float32)
        ahead = lax.dot_general(lower, onehot, NN, preferred_element_type=jnp.float32)
        before = lax.dot_general(ahead.astype(bf16), ones, NN, preferred_element_type=jnp.float32)
        return jnp.where(mask, within + before, rank)

    rank = lax.fori_loop(0, peers, ranked, jnp.zeros(target.shape, jnp.float32)).astype(jnp.int32)
    halves = (rows + 1) // 2
    wide = lax.div(rank, 2 * LANES)
    within = rank - 2 * LANES * wide
    right_half = (within >= LANES).astype(jnp.int32)
    slot_ref[0] = jnp.where(target < 0, -1, target * rows + right_half * halves + wide)
    slot_ref[1] = within - LANES * right_half
    slot_ref[2] = jnp.where(target < 0, -1, target * halves + wide)
    slot_ref[3] = within
    height = left_ref.shape[0] // 15

    def place(chunk, carry):
        at = pl.ds(pl.multiple_of(chunk * LANES, LANES), LANES)
        high_mask = iota((height, LANES), 0) == slot_ref[2, pl.ds(chunk, 1), :]
        low_mask = iota((2 * LANES, LANES), 0) == slot_ref[3, pl.ds(chunk, 1), :]
        right_ref[:, at] = low_mask.astype(jnp.float32).astype(bf16)
        values = payload_ref[:, at]
        first = values.astype(bf16).astype(jnp.float32)
        rest = values - first
        second = rest.astype(bf16).astype(jnp.float32)
        third = rest - second
        piece = 0
        for row in range(6):
            for part in (first, second, third)[: 2 if row < 3 else 3]:
                left_ref[piece * height : (piece + 1) * height, at] = jnp.where(
                    high_mask, part[row : row + 1, :], 0.0
                ).astype(bf16)
                piece += 1
        return carry

    lax.fori_loop(0, chunks, place, 0)
    placed = lax.dot_general(
        left_ref[...], right_ref[...], NT, preferred_element_type=jnp.float32
    )
    piece = 0
    for row in range(6):
        count = 2 if row < 3 else 3
        total = placed[piece * height : (piece + 1) * height]
        for more in range(1, count):
            total = total + placed[(piece + more) * height : (piece + more + 1) * height]
        piece += count
        for peer in range(peers):
            first, middle = peer * halves, row * rows + halves
            sent_ref[peer, row * rows : middle, :] = total[first : first + halves, :LANES]
            if rows > halves:
                sent_ref[peer, middle : (row + 1) * rows, :] = total[
                    first : first + rows - halves, LANES:
                ]


def stencil(position):
    base = jnp.floor(position)
    angle = (0.5 * math.pi) * (position - base)
    sine, cosine = jnp.sin(angle), jnp.cos(angle)
    weights = [0.25 - 0.25 * sine, 0.25 + 0.25 * cosine, 0.25 + 0.25 * sine, 0.25 - 0.25 * cosine]
    return base.astype(jnp.int32), weights


def node_weights(size, base, weights, row):
    step = iota((size, LANES), 0) - base[row : row + 1, :]
    result = jnp.zeros((size, LANES), jnp.float32)
    for index in range(4):
        result = jnp.where(step == index - 1, weights[index][row : row + 1, :], result)
    return result


def spread_build(sizes, rows, block, left_ref, right_ref):
    size_x, size_y, size_z = sizes
    height = 3 * size_x * size_y
    base, weights = stencil(block[3 * rows : 6 * rows])
    for k in range(rows):
        at = slice(k * LANES, (k + 1) * LANES)
        along_x = node_weights(size_x, base, weights, k)
        along_y = node_weights(size_y, base, weights, rows + k)
        high, low = split_two(node_weights(size_z, base, weights, 2 * rows + k))
        right_ref[:size_z, at] = high
        right_ref[size_z:, at] = low
        for dimension in range(3):
            scaled = along_x * block[dimension * rows + k : dimension * rows + k + 1, :]
            for x in range(size_x):
                first = (dimension * size_x + x) * size_y
                high, low = split_two(along_y * scaled[x : x + 1, :])
                left_ref[first : first + size_y, at] = high
                left_ref[height + first : height + first + size_y, at] = low


def spread_add(left_ref, right_ref, total_ref):
    total_ref[...] += lax.dot_general(
        left_ref[...], right_ref[...], NT, preferred_element_type=jnp.float32
    )


def outward_kernel(
    peers, rows, sizes, target_ref, payload_ref, field_ref, slot_ref, position_ref,
    route_left, route_right, sent_ref, arrived_ref, left_ref, right_ref, left_other, right_other, total_ref,
    send_sem, recv_sem,
):
    me = lax.axis_index(PEERS)
    size_z = sizes[2]
    height = 3 * sizes[0] * sizes[1]
    barrier = greet_peers(peers)
    route_part(peers, rows, target_ref, payload_ref, sent_ref, slot_ref, route_left, route_right)
    pl.semaphore_wait(barrier, peers - 1)
    copy = exchange(peers, sent_ref, arrived_ref, send_sem, recv_sem)

    def send(step, carry):
        copy(step).start()
        return carry

    lax.fori_loop(1, peers, send, 0)
    total_ref[...] = jnp.zeros_like(total_ref)

    buffers = [(left_ref, right_ref), (left_other, right_other)]

    def build(source, block, buffer):
        position_ref[source] = block[3 * rows : 6 * rows]
        spread_build(sizes, rows, block, *buffer)

    def one(step, built):
        copy(step).wait_recv()
        source = lax.rem(me + peers - step, peers)
        spread_add(*buffers[built], total_ref)
        build(source, arrived_ref[source], buffers[1 - built])

    def two(pair, carry):
        one(2 * pair + 1, 0)
        one(2 * pair + 2, 1)
        return carry

    build(me, sent_ref[me], buffers[0])
    lax.fori_loop(0, (peers - 1) // 2, two, 0)
    if peers % 2 == 0:
        one(peers - 1, 0)
    spread_add(*buffers[1 - peers % 2], total_ref)
    field_ref[...] = (total_ref[height:, size_z:] + total_ref[height:, :size_z]) + (
        total_ref[:height, size_z:] + total_ref[:height, :size_z]
    )

    def finish(step, carry):
        copy(step).wait_send()
        return carry

    lax.fori_loop(1, peers, finish, 0)


def outward(target, payload, peers, rows, sizes):
    chunks = target.shape[0]
    slots_high = -(-peers * ((rows + 1) // 2) // 16) * 16
    height = 3 * sizes[0] * sizes[1]
    return pl.pallas_call(
        lambda *refs: outward_kernel(peers, rows, sizes, *refs),
        out_shape=(
            jax.ShapeDtypeStruct((height, sizes[2]), jnp.float32),
            jax.ShapeDtypeStruct((4, chunks, LANES), jnp.int32),
            jax.ShapeDtypeStruct((peers, 3 * rows, LANES), jnp.float32),
        ),
        in_specs=[pl.BlockSpec(memory_space=pltpu.VMEM)] * 2,
        out_specs=(pl.BlockSpec(memory_space=pltpu.VMEM),) * 3,
        scratch_shapes=[
            pltpu.VMEM((15 * slots_high, chunks * LANES), jnp.bfloat16),
            pltpu.VMEM((2 * LANES, chunks * LANES), jnp.bfloat16),
            pltpu.VMEM((peers, 6 * rows, LANES), jnp.float32),
            pltpu.VMEM((peers, 6 * rows, LANES), jnp.float32),
            pltpu.VMEM((2 * height, rows * LANES), jnp.bfloat16),
            pltpu.VMEM((2 * sizes[2], rows * LANES), jnp.bfloat16),
            pltpu.VMEM((2 * height, rows * LANES), jnp.bfloat16),
            pltpu.VMEM((2 * sizes[2], rows * LANES), jnp.bfloat16),
            pltpu.VMEM((2 * height, 2 * sizes[2]), jnp.float32),
            pltpu.SemaphoreType.DMA((peers,)),
            pltpu.SemaphoreType.DMA((peers,)),
        ],
        compiler_params=pltpu.CompilerParams(
            vmem_limit_bytes=VMEM_LIMIT, collective_id=0, has_side_effects=True
        ),
        name="outward",
    )(target, payload)


def sample_part(sizes, rows, position, left_ref, right_ref, part_ref):
    size_x, size_y, size_z = sizes
    base, weights = stencil(position)
    for k in range(rows):
        at = slice(k * LANES, (k + 1) * LANES)
        high, low = split_two(node_weights(size_z, base, weights, 2 * rows + k))
        right_ref[:size_z, at] = high
        right_ref[size_z : 2 * size_z, at] = high
        right_ref[2 * size_z :, at] = low
    part_ref[...] = lax.dot_general(
        left_ref[...], right_ref[...], NN, preferred_element_type=jnp.float32
    )
    result = [[], [], []]
    for k in range(rows):
        at = slice(k * LANES, (k + 1) * LANES)
        along_x = node_weights(size_x, base, weights, k)
        along_y = node_weights(size_y, base, weights, rows + k)
        for dimension in range(3):
            total = jnp.zeros((size_y, LANES), jnp.float32)
            for x in range(size_x):
                first = (dimension * size_x + x) * size_y
                total = total + along_x[x : x + 1, :] * part_ref[first : first + size_y, at]
            result[dimension].append(jnp.sum(total * along_y, axis=0, keepdims=True))
    return jnp.concatenate(result[0] + result[1] + result[2], axis=0) / VELOCITY_UNIT


def collect_part(peers, rows, returned_ref, slot_ref, result_ref, table_ref, left_ref):
    height = left_ref.shape[0] // 3
    markers = result_ref.shape[1]
    table_ref[...] = jnp.zeros_like(table_ref)
    for row in range(3):
        for peer in range(peers):
            first = row * height + peer * rows
            table_ref[first : first + rows, :] = returned_ref[peer, row * rows : (row + 1) * rows, :]
    high, low = split_two(table_ref[...])
    left_ref[:, :LANES] = high
    left_ref[:, LANES:] = low

    def one(chunk, count):
        width = count * LANES
        wide = [
            jnp.concatenate([slot_ref[part, pl.ds(chunk + j, 1), :] for j in range(count)], axis=1)
            for part in range(2)
        ]
        low_mask = iota((LANES, width), 0) == wide[1]
        onehot = low_mask.astype(jnp.float32).astype(jnp.bfloat16)
        found = lax.dot_general(
            left_ref[...],
            jnp.concatenate([onehot, onehot], axis=0),
            NN,
            preferred_element_type=jnp.float32,
        )
        high_mask = iota((height, width), 0) == wide[0]
        return jnp.concatenate(
            [
                jnp.sum(
                    jnp.where(high_mask, found[row * height : (row + 1) * height], 0.0),
                    axis=0,
                    keepdims=True,
                )
                for row in range(3)
            ],
            axis=0,
        )

    whole, rest = markers // LANES, markers % LANES

    def step(pair, carry):
        at = pl.ds(pl.multiple_of(2 * pair * LANES, 2 * LANES), 2 * LANES)
        result_ref[:, at] = one(2 * pair, 2)
        return carry

    lax.fori_loop(0, whole // 2, step, 0, unroll=2)
    if whole % 2:
        result_ref[:, (whole - 1) * LANES : whole * LANES] = one(whole - 1, 1)
    if rest:
        result_ref[:, markers - rest :] = one(whole, 1)[:, :rest]


def homeward_kernel(
    peers, rows, sizes, position_ref, velocity_ref, slot_ref, result_ref,
    sampled_ref, returned_ref, left_ref, right_ref, part_ref, table_ref, table_left,
    send_sem, recv_sem,
):
    me = lax.axis_index(PEERS)
    size_z = sizes[2]
    barrier = greet_peers(peers)
    high, low = split_two(velocity_ref[...])
    left_ref[:, :size_z] = high
    left_ref[:, size_z : 2 * size_z] = low
    left_ref[:, 2 * size_z :] = high
    pl.semaphore_wait(barrier, peers - 1)
    copy = exchange(peers, sampled_ref, returned_ref, send_sem, recv_sem)

    def one(step, carry):
        peer = lax.rem(me + step, peers)
        sampled_ref[peer] = sample_part(
            sizes, rows, position_ref[peer], left_ref, right_ref, part_ref
        )
        copy(step).start()
        return carry

    lax.fori_loop(1, peers, one, 0)
    returned_ref[me] = sample_part(sizes, rows, position_ref[me], left_ref, right_ref, part_ref)

    def finish(step, carry):
        copy(step).wait_recv()
        copy(step).wait_send()
        return carry

    lax.fori_loop(1, peers, finish, 0)
    collect_part(peers, rows, returned_ref, slot_ref, result_ref, table_ref, table_left)


def homeward(position, velocity, slots, markers, rows, sizes):
    peers = position.shape[0]
    slots_high = -(-peers * rows // 16) * 16
    height = 3 * sizes[0] * sizes[1]
    return pl.pallas_call(
        lambda *refs: homeward_kernel(peers, rows, sizes, *refs),
        out_shape=jax.ShapeDtypeStruct((3, markers), jnp.float32),
        in_specs=[pl.BlockSpec(memory_space=pltpu.VMEM)] * 3,
        out_specs=pl.BlockSpec(memory_space=pltpu.VMEM),
        scratch_shapes=[
            pltpu.VMEM((peers, 3 * rows, LANES), jnp.float32),
            pltpu.VMEM((peers, 3 * rows, LANES), jnp.float32),
            pltpu.VMEM((height, 3 * sizes[2]), jnp.bfloat16),
            pltpu.VMEM((3 * sizes[2], rows * LANES), jnp.bfloat16),
            pltpu.VMEM((height, rows * LANES), jnp.float32),
            pltpu.VMEM((3 * slots_high, LANES), jnp.float32),
            pltpu.VMEM((3 * slots_high, 2 * LANES), jnp.bfloat16),
            pltpu.SemaphoreType.DMA((peers,)),
            pltpu.SemaphoreType.DMA((peers,)),
        ],
        compiler_params=pltpu.CompilerParams(
            vmem_limit_bytes=VMEM_LIMIT, collective_id=1, has_side_effects=True
        ),
        name="homeward",
    )(position, velocity, slots)


def shards(populations, displacement, stiffness, base_node, offset, destination):
    size_x, size_y, size_z = (populations.shape[1], populations.shape[2], populations.shape[3])
    peer_count = lax.axis_size(("gz", "gy"))
    markers = displacement.shape[1]
    capacity = max(2, (2 * markers + peer_count - 1) // peer_count)
    rows = -(-capacity // LANES)
    chunks = -(-markers // LANES)
    spare = chunks * LANES - markers
    sizes = (size_x, size_y, size_z)
    forces = marker_forces(displacement, stiffness)
    position = base_node.astype(jnp.float32) + offset
    target = jnp.pad(destination[:, 0], (0, spare), constant_values=-1).reshape(chunks, LANES)
    payload = jnp.pad(jnp.concatenate([forces, position], axis=0), ((0, 0), (0, spare)))
    field, slots, marker_position = outward(target, payload, peer_count, rows, sizes)
    force_field = field.reshape(3, size_x, size_y, size_z)
    new_populations, velocity = fluid(populations, force_field)
    velocity = velocity.reshape(3 * size_x * size_y, size_z)
    marker_velocity = homeward(marker_position, velocity, slots, markers, rows, sizes)
    return (new_populations, marker_velocity)


def solution(mesh):
    return jax.shard_map(
        shards,
        mesh=mesh,
        in_specs=(
            P(None, ("groups", "gx"), "gy", "gz"),
            P(None, ("groups", "gz", "gy", "gx")),
            P(("groups", "gz", "gy", "gx")),
            P(None, ("groups", "gz", "gy", "gx")),
            P(None, ("groups", "gz", "gy", "gx")),
            P(("groups", "gz", "gy", "gx"), None),
        ),
        out_specs=(P(None, ("groups", "gx"), "gy", "gz"), P(None, ("groups", "gz", "gy", "gx"))),
        check_vma=False,
    )
```

```python
import math

import jax
import jax.numpy as jnp
import numpy as np
from jax import lax
from jax.experimental import pallas as pl
from jax.experimental.pallas import tpu as pltpu
from jax.sharding import PartitionSpec as P

LATTICE = np.array(
    [
        [0, 0, 0],
        [1, 0, 0],
        [-1, 0, 0],
        [0, 1, 0],
        [0, -1, 0],
        [0, 0, 1],
        [0, 0, -1],
        [1, 1, 0],
        [-1, -1, 0],
        [1, -1, 0],
        [-1, 1, 0],
        [1, 0, 1],
        [-1, 0, -1],
        [1, 0, -1],
        [-1, 0, 1],
        [0, 1, 1],
        [0, -1, -1],
        [0, 1, -1],
        [0, -1, 1],
    ]
)
WEIGHTS = [1.0 / 3.0] + [1.0 / 18.0] * 6 + [1.0 / 36.0] * 12
RELAXATION = 0.8
VELOCITY_UNIT = 0.01
MESH = pl.DeviceIdType.MESH


def marker_forces(displacement, stiffness):
    grouped = displacement.reshape(3, stiffness.shape[0], -1)
    centred = grouped - jnp.mean(grouped, axis=2, keepdims=True)
    return (stiffness[None, :, None] * centred).reshape(3, -1)


def momentum_sum(populations, dimension):
    total = jnp.zeros_like(populations[0])
    for index in range(19):
        step_sign = int(LATTICE[index][dimension])
        if step_sign != 0:
            total = total + step_sign * populations[index]
    return total


def collide(populations, force_field):
    density = sum(populations[1:], populations[0])
    velocity = [
        (momentum_sum(populations, dimension) + 0.5 * force_field[dimension]) / density
        for dimension in range(3)
    ]
    speed_squared = (
        velocity[0] * velocity[0] + velocity[1] * velocity[1] + velocity[2] * velocity[2]
    )
    factor = 1.0 - 0.5 / RELAXATION
    result = []
    for index in range(19):
        lattice_row = [int(value) for value in LATTICE[index]]
        along = jnp.zeros_like(density)
        for dimension in range(3):
            if lattice_row[dimension] != 0:
                along = along + lattice_row[dimension] * velocity[dimension]
        equilibrium = (
            WEIGHTS[index]
            * density
            * (1.0 + 3.0 * along + 4.5 * along * along - 1.5 * speed_squared)
        )
        source = jnp.zeros_like(density)
        for dimension in range(3):
            source = (
                source
                + (
                    3.0 * (lattice_row[dimension] - velocity[dimension])
                    + 9.0 * along * lattice_row[dimension]
                )
                * force_field[dimension]
            )
        result.append(
            populations[index]
            - (populations[index] - equilibrium) / RELAXATION
            + factor * WEIGHTS[index] * source
        )
    return result


def directions(dimension, sign):
    return [index for index in range(19) if int(LATTICE[index][dimension]) == sign]


AXES = ("gx", "gy", "gz")
FACES = [(dimension, sign) for dimension in range(3) for sign in (1, -1)]


def neighbour(dimension, sign):
    size = lax.axis_size(AXES[dimension])
    return {AXES[dimension]: lax.rem(lax.axis_index(AXES[dimension]) + size + sign, size)}


def fluid_kernel(
    populations_ref, field_ref, result_ref, velocity_ref,
    out_x, out_y, out_z, in_x, in_y, in_z, send_sem, recv_sem,
):
    size_x, size_y, size_z = populations_ref.shape[1:]
    barrier = pltpu.get_barrier_semaphore()
    for face in FACES:
        pl.semaphore_signal(barrier, inc=1, device_id=neighbour(*face), device_id_type=MESH)

    def collided(x):
        return collide(
            [populations_ref[index, x] for index in range(19)],
            [field_ref[dimension, x] for dimension in range(3)],
        )

    def copy(face, source, target):
        dimension, sign = FACES[face]
        return pltpu.make_async_remote_copy(
            src_ref=source.at[face % 2],
            dst_ref=target.at[face % 2],
            send_sem=send_sem.at[face],
            recv_sem=recv_sem.at[face],
            device_id=neighbour(dimension, sign),
            device_id_type=MESH,
        )

    first, last = collided(0), collided(size_x - 1)
    for slot, index in enumerate(directions(0, 1)):
        out_x[0, slot] = last[index]
        result_ref[index, 1] = first[index]
    for slot, index in enumerate(directions(0, -1)):
        out_x[1, slot] = first[index]
        result_ref[index, size_x - 2] = last[index]
    for index in directions(0, 0):
        result_ref[index, 0] = first[index]
        result_ref[index, size_x - 1] = last[index]
    pl.semaphore_wait(barrier, len(FACES))
    copies = [copy(face, out_x, in_x) for face in (0, 1)]
    for one in copies:
        one.start()

    def inner(x, carry):
        post = collided(x)
        for index in range(19):
            result_ref[index, x + int(LATTICE[index][0])] = post[index]
        return carry

    lax.fori_loop(1, size_x - 1, inner, 0)
    for one in copies:
        one.wait_recv()
    for slot, index in enumerate(directions(0, 1)):
        result_ref[index, 0] = in_x[0, slot]
    for slot, index in enumerate(directions(0, -1)):
        result_ref[index, size_x - 1] = in_x[1, slot]

    for side, sign in enumerate((1, -1)):
        edge = size_y - 1 if sign == 1 else 0
        for slot, index in enumerate(directions(1, sign)):
            out_y[side, slot] = jnp.concatenate(
                [result_ref[index, x, edge : edge + 1, :] for x in range(size_x)], axis=0
            )
    copies_y = [copy(face, out_y, in_y) for face in (2, 3)]
    for one in copies_y:
        one.start()
    for one in copies_y:
        one.wait_recv()
    for side, sign in enumerate((1, -1)):
        for slot, index in enumerate(directions(1, sign)):
            for x in range(size_x):
                plane = result_ref[index, x]
                row = in_y[side, slot, x : x + 1, :]
                result_ref[index, x] = jnp.concatenate(
                    [row, plane[: size_y - 1]] if sign == 1 else [plane[1:], row], axis=0
                )

    lane = iota((size_y, size_z), 1)
    for side, sign in enumerate((1, -1)):
        edge = size_z - 1 if sign == 1 else 0
        packed = jnp.zeros((size_y, size_z), jnp.float32)
        for slot, index in enumerate(directions(2, sign)):
            for x in range(size_x):
                packed = jnp.where(
                    lane == slot * size_x + x, result_ref[index, x, :, edge : edge + 1], packed
                )
        out_z[side] = packed
    copies_z = [copy(face, out_z, in_z) for face in (4, 5)]
    for one in copies_z:
        one.start()
    for one in copies_z:
        one.wait_recv()
    for side, sign in enumerate((1, -1)):
        edge = 0 if sign == 1 else size_z - 1
        arrived = in_z[side]
        for slot, index in enumerate(directions(2, sign)):
            for x in range(size_x):
                at = slot * size_x + x
                turned = pltpu.roll(result_ref[index, x], 1 if sign == 1 else size_z - 1, axis=1)
                result_ref[index, x] = jnp.where(lane == edge, arrived[:, at : at + 1], turned)

    def speed(x, carry):
        planes = [result_ref[index, x] for index in range(19)]
        density = sum(planes[1:], planes[0])
        for dimension in range(3):
            velocity_ref[dimension, x] = momentum_sum(planes, dimension) / density
        return carry

    lax.fori_loop(0, size_x, speed, 0, unroll=2)
    for one in copies + copies_y + copies_z:
        one.wait_send()


def fluid(populations, force_field):
    size_x, size_y, size_z = populations.shape[1:]
    moving = len(directions(0, 1))
    assert moving * size_x <= size_z
    faces = [
        (2, moving, size_y, size_z),
        (2, moving, size_x, size_z),
        (2, size_y, size_z),
    ]
    return pl.pallas_call(
        fluid_kernel,
        out_shape=(
            jax.ShapeDtypeStruct(populations.shape, jnp.float32),
            jax.ShapeDtypeStruct((3, size_x, size_y, size_z), jnp.float32),
        ),
        in_specs=[pl.BlockSpec(memory_space=pltpu.VMEM)] * 2,
        out_specs=(pl.BlockSpec(memory_space=pltpu.VMEM),) * 2,
        scratch_shapes=[pltpu.VMEM(shape, jnp.float32) for shape in faces + faces]
        + [pltpu.SemaphoreType.DMA((len(FACES),)), pltpu.SemaphoreType.DMA((len(FACES),))],
        compiler_params=pltpu.CompilerParams(
            vmem_limit_bytes=VMEM_LIMIT, collective_id=2, has_side_effects=True
        ),
        name="fluid",
    )(populations, force_field)


LANES = 128
VMEM_LIMIT = 48 * 1024 * 1024
NT = (((1,), (1,)), ((), ()))
NN = (((1,), (0,)), ((), ()))


def iota(shape, dimension):
    return lax.broadcasted_iota(jnp.int32, shape, dimension)


def split_two(value):
    high = value.astype(jnp.bfloat16)
    return high, (value - high.astype(jnp.float32)).astype(jnp.bfloat16)


PEERS = ("gz", "gy")


def peer_device(peer):
    across = lax.axis_size("gy")
    return {"gz": lax.div(peer, across), "gy": lax.rem(peer, across)}


def exchange(peers, sent_ref, received_ref, send_sem, recv_sem):
    me = lax.axis_index(PEERS)

    def copy(step):
        peer = lax.rem(me + step, peers)
        return pltpu.make_async_remote_copy(
            src_ref=sent_ref.at[peer],
            dst_ref=received_ref.at[me],
            send_sem=send_sem.at[step],
            recv_sem=recv_sem.at[step],
            device_id=peer_device(peer),
            device_id_type=MESH,
        )

    return copy


def greet_peers(peers):
    me = lax.axis_index(PEERS)
    barrier = pltpu.get_barrier_semaphore()

    def greet(step, carry):
        pl.semaphore_signal(
            barrier, inc=1, device_id=peer_device(lax.rem(me + step, peers)), device_id_type=MESH
        )
        return carry

    lax.fori_loop(1, peers, greet, 0)
    return barrier


def route_part(peers, rows, target_ref, payload_ref, sent_ref, slot_ref, left_ref, right_ref):
    chunks = target_ref.shape[0]
    target = target_ref[...]
    bf16 = jnp.bfloat16
    upper = (iota((LANES, LANES), 0) < iota((LANES, LANES), 1)).astype(bf16)
    lower = (iota((chunks, chunks), 1) < iota((chunks, chunks), 0)).astype(bf16)
    ones = jnp.ones((LANES, LANES), bf16)

    def ranked(peer, rank):
        mask = target == peer
        onehot = mask.astype(jnp.float32).astype(bf16)
        within = lax.dot_general(onehot, upper, NN, preferred_element_type=jnp.float32)
        ahead = lax.dot_general(lower, onehot, NN, preferred_element_type=jnp.float32)
        before = lax.dot_general(ahead.astype(bf16), ones, NN, preferred_element_type=jnp.float32)
        return jnp.where(mask, within + before, rank)

    rank = lax.fori_loop(0, peers, ranked, jnp.zeros(target.shape, jnp.float32)).astype(jnp.int32)
    halves = (rows + 1) // 2
    wide = lax.div(rank, 2 * LANES)
    within = rank - 2 * LANES * wide
    right_half = (within >= LANES).astype(jnp.int32)
    slot_ref[0] = jnp.where(target < 0, -1, target * rows + right_half * halves + wide)
    slot_ref[1] = within - LANES * right_half
    slot_ref[2] = jnp.where(target < 0, -1, target * halves + wide)
    slot_ref[3] = within
    height = left_ref.shape[0] // 15

    def place(chunk, carry):
        at = pl.ds(pl.multiple_of(chunk * LANES, LANES), LANES)
        high_mask = iota((height, LANES), 0) == slot_ref[2, pl.ds(chunk, 1), :]
        low_mask = iota((2 * LANES, LANES), 0) == slot_ref[3, pl.ds(chunk, 1), :]
        right_ref[:, at] = low_mask.astype(jnp.float32).astype(bf16)
        values = payload_ref[:, at]
        first = values.astype(bf16).astype(jnp.float32)
        rest = values - first
        second = rest.astype(bf16).astype(jnp.float32)
        third = rest - second
        piece = 0
        for row in range(6):
            for part in (first, second, third)[: 2 if row < 3 else 3]:
                left_ref[piece * height : (piece + 1) * height, at] = jnp.where(
                    high_mask, part[row : row + 1, :], 0.0
                ).astype(bf16)
                piece += 1
        return carry

    lax.fori_loop(0, chunks, place, 0, unroll=4)
    placed = lax.dot_general(
        left_ref[...], right_ref[...], NT, preferred_element_type=jnp.float32
    )
    piece = 0
    for row in range(6):
        count = 2 if row < 3 else 3
        total = placed[piece * height : (piece + 1) * height]
        for more in range(1, count):
            total = total + placed[(piece + more) * height : (piece + more + 1) * height]
        piece += count
        for peer in range(peers):
            first, middle = peer * halves, row * rows + halves
            sent_ref[peer, row * rows : middle, :] = total[first : first + halves, :LANES]
            if rows > halves:
                sent_ref[peer, middle : (row + 1) * rows, :] = total[
                    first : first + rows - halves, LANES:
                ]


def stencil(position):
    base = jnp.floor(position)
    angle = (0.5 * math.pi) * (position - base)
    sine, cosine = jnp.sin(angle), jnp.cos(angle)
    weights = [0.25 - 0.25 * sine, 0.25 + 0.25 * cosine, 0.25 + 0.25 * sine, 0.25 - 0.25 * cosine]
    return base.astype(jnp.int32), weights


def node_weights(size, base, weights, row):
    step = iota((size, LANES), 0) - base[row : row + 1, :]
    result = jnp.zeros((size, LANES), jnp.float32)
    for index in range(4):
        result = jnp.where(step == index - 1, weights[index][row : row + 1, :], result)
    return result


def spread_build(sizes, rows, block, left_ref, right_ref):
    size_x, size_y, size_z = sizes
    height = 3 * size_x * size_y
    base, weights = stencil(block[3 * rows : 6 * rows])
    for k in range(rows):
        at = slice(k * LANES, (k + 1) * LANES)
        along_x = node_weights(size_x, base, weights, k)
        along_y = node_weights(size_y, base, weights, rows + k)
        high, low = split_two(node_weights(size_z, base, weights, 2 * rows + k))
        right_ref[:size_z, at] = high
        right_ref[size_z:, at] = low
        for dimension in range(3):
            scaled = along_x * block[dimension * rows + k : dimension * rows + k + 1, :]
            for x in range(size_x):
                first = (dimension * size_x + x) * size_y
                high, low = split_two(along_y * scaled[x : x + 1, :])
                left_ref[first : first + size_y, at] = high
                left_ref[height + first : height + first + size_y, at] = low


def spread_add(left_ref, right_ref, total_ref):
    total_ref[...] += lax.dot_general(
        left_ref[...], right_ref[...], NT, preferred_element_type=jnp.float32
    )


def outward_kernel(
    peers, rows, sizes, target_ref, payload_ref, field_ref, slot_ref, position_ref,
    route_left, route_right, sent_ref, arrived_ref, left_ref, right_ref, left_other, right_other, total_ref,
    send_sem, recv_sem,
):
    me = lax.axis_index(PEERS)
    size_z = sizes[2]
    height = 3 * sizes[0] * sizes[1]
    barrier = greet_peers(peers)
    route_part(peers, rows, target_ref, payload_ref, sent_ref, slot_ref, route_left, route_right)
    pl.semaphore_wait(barrier, peers - 1)
    copy = exchange(peers, sent_ref, arrived_ref, send_sem, recv_sem)

    def send(step, carry):
        copy(step).start()
        return carry

    lax.fori_loop(1, peers, send, 0)
    total_ref[...] = jnp.zeros_like(total_ref)

    buffers = [(left_ref, right_ref), (left_other, right_other)]

    def build(source, block, buffer):
        position_ref[source] = block[3 * rows : 6 * rows]
        spread_build(sizes, rows, block, *buffer)

    def one(step, built):
        copy(step).wait_recv()
        source = lax.rem(me + peers - step, peers)
        spread_add(*buffers[built], total_ref)
        build(source, arrived_ref[source], buffers[1 - built])

    def two(pair, carry):
        one(2 * pair + 1, 0)
        one(2 * pair + 2, 1)
        return carry

    build(me, sent_ref[me], buffers[0])
    lax.fori_loop(0, (peers - 1) // 2, two, 0)
    if peers % 2 == 0:
        one(peers - 1, 0)
    spread_add(*buffers[1 - peers % 2], total_ref)
    field_ref[...] = (total_ref[height:, size_z:] + total_ref[height:, :size_z]) + (
        total_ref[:height, size_z:] + total_ref[:height, :size_z]
    )

    def finish(step, carry):
        copy(step).wait_send()
        return carry

    lax.fori_loop(1, peers, finish, 0)


def outward(target, payload, peers, rows, sizes):
    chunks = target.shape[0]
    slots_high = -(-peers * ((rows + 1) // 2) // 16) * 16
    height = 3 * sizes[0] * sizes[1]
    return pl.pallas_call(
        lambda *refs: outward_kernel(peers, rows, sizes, *refs),
        out_shape=(
            jax.ShapeDtypeStruct((height, sizes[2]), jnp.float32),
            jax.ShapeDtypeStruct((4, chunks, LANES), jnp.int32),
            jax.ShapeDtypeStruct((peers, 3 * rows, LANES), jnp.float32),
        ),
        in_specs=[pl.BlockSpec(memory_space=pltpu.VMEM)] * 2,
        out_specs=(pl.BlockSpec(memory_space=pltpu.VMEM),) * 3,
        scratch_shapes=[
            pltpu.VMEM((15 * slots_high, chunks * LANES), jnp.bfloat16),
            pltpu.VMEM((2 * LANES, chunks * LANES), jnp.bfloat16),
            pltpu.VMEM((peers, 6 * rows, LANES), jnp.float32),
            pltpu.VMEM((peers, 6 * rows, LANES), jnp.float32),
            pltpu.VMEM((2 * height, rows * LANES), jnp.bfloat16),
            pltpu.VMEM((2 * sizes[2], rows * LANES), jnp.bfloat16),
            pltpu.VMEM((2 * height, rows * LANES), jnp.bfloat16),
            pltpu.VMEM((2 * sizes[2], rows * LANES), jnp.bfloat16),
            pltpu.VMEM((2 * height, 2 * sizes[2]), jnp.float32),
            pltpu.SemaphoreType.DMA((peers,)),
            pltpu.SemaphoreType.DMA((peers,)),
        ],
        compiler_params=pltpu.CompilerParams(
            vmem_limit_bytes=VMEM_LIMIT, collective_id=0, has_side_effects=True
        ),
        name="outward",
    )(target, payload)


def sample_part(sizes, rows, position, left_ref, right_ref, part_ref):
    size_x, size_y, size_z = sizes
    base, weights = stencil(position)
    for k in range(rows):
        at = slice(k * LANES, (k + 1) * LANES)
        high, low = split_two(node_weights(size_z, base, weights, 2 * rows + k))
        right_ref[:size_z, at] = high
        right_ref[size_z : 2 * size_z, at] = high
        right_ref[2 * size_z :, at] = low
    part_ref[...] = lax.dot_general(
        left_ref[...], right_ref[...], NN, preferred_element_type=jnp.float32
    )
    result = [[], [], []]
    for k in range(rows):
        at = slice(k * LANES, (k + 1) * LANES)
        along_x = node_weights(size_x, base, weights, k)
        along_y = node_weights(size_y, base, weights, rows + k)
        for dimension in range(3):
            total = jnp.zeros((size_y, LANES), jnp.float32)
            for x in range(size_x):
                first = (dimension * size_x + x) * size_y
                total = total + along_x[x : x + 1, :] * part_ref[first : first + size_y, at]
            result[dimension].append(jnp.sum(total * along_y, axis=0, keepdims=True))
    return jnp.concatenate(result[0] + result[1] + result[2], axis=0) / VELOCITY_UNIT


def collect_part(peers, rows, returned_ref, slot_ref, result_ref, table_ref, left_ref):
    height = left_ref.shape[0] // 3
    markers = result_ref.shape[1]
    table_ref[...] = jnp.zeros_like(table_ref)
    for row in range(3):
        for peer in range(peers):
            first = row * height + peer * rows
            table_ref[first : first + rows, :] = returned_ref[peer, row * rows : (row + 1) * rows, :]
    high, low = split_two(table_ref[...])
    left_ref[:, :LANES] = high
    left_ref[:, LANES:] = low

    def one(chunk, count):
        width = count * LANES
        wide = [
            jnp.concatenate([slot_ref[part, pl.ds(chunk + j, 1), :] for j in range(count)], axis=1)
            for part in range(2)
        ]
        low_mask = iota((LANES, width), 0) == wide[1]
        onehot = low_mask.astype(jnp.float32).astype(jnp.bfloat16)
        found = lax.dot_general(
            left_ref[...],
            jnp.concatenate([onehot, onehot], axis=0),
            NN,
            preferred_element_type=jnp.float32,
        )
        high_mask = iota((height, width), 0) == wide[0]
        return jnp.concatenate(
            [
                jnp.sum(
                    jnp.where(high_mask, found[row * height : (row + 1) * height], 0.0),
                    axis=0,
                    keepdims=True,
                )
                for row in range(3)
            ],
            axis=0,
        )

    whole, rest = markers // LANES, markers % LANES

    def step(pair, carry):
        at = pl.ds(pl.multiple_of(2 * pair * LANES, 2 * LANES), 2 * LANES)
        result_ref[:, at] = one(2 * pair, 2)
        return carry

    lax.fori_loop(0, whole // 2, step, 0, unroll=4)
    if whole % 2:
        result_ref[:, (whole - 1) * LANES : whole * LANES] = one(whole - 1, 1)
    if rest:
        result_ref[:, markers - rest :] = one(whole, 1)[:, :rest]


def homeward_kernel(
    peers, rows, sizes, position_ref, velocity_ref, slot_ref, result_ref,
    sampled_ref, returned_ref, left_ref, right_ref, part_ref, table_ref, table_left,
    send_sem, recv_sem,
):
    me = lax.axis_index(PEERS)
    size_z = sizes[2]
    barrier = greet_peers(peers)
    high, low = split_two(velocity_ref[...])
    left_ref[:, :size_z] = high
    left_ref[:, size_z : 2 * size_z] = low
    left_ref[:, 2 * size_z :] = high
    pl.semaphore_wait(barrier, peers - 1)
    copy = exchange(peers, sampled_ref, returned_ref, send_sem, recv_sem)

    def one(step, carry):
        peer = lax.rem(me + step, peers)
        sampled_ref[peer] = sample_part(
            sizes, rows, position_ref[peer], left_ref, right_ref, part_ref
        )
        copy(step).start()
        return carry

    lax.fori_loop(1, peers, one, 0)
    returned_ref[me] = sample_part(sizes, rows, position_ref[me], left_ref, right_ref, part_ref)

    def finish(step, carry):
        copy(step).wait_recv()
        copy(step).wait_send()
        return carry

    lax.fori_loop(1, peers, finish, 0)
    collect_part(peers, rows, returned_ref, slot_ref, result_ref, table_ref, table_left)


def homeward(position, velocity, slots, markers, rows, sizes):
    peers = position.shape[0]
    slots_high = -(-peers * rows // 16) * 16
    height = 3 * sizes[0] * sizes[1]
    return pl.pallas_call(
        lambda *refs: homeward_kernel(peers, rows, sizes, *refs),
        out_shape=jax.ShapeDtypeStruct((3, markers), jnp.float32),
        in_specs=[pl.BlockSpec(memory_space=pltpu.VMEM)] * 3,
        out_specs=pl.BlockSpec(memory_space=pltpu.VMEM),
        scratch_shapes=[
            pltpu.VMEM((peers, 3 * rows, LANES), jnp.float32),
            pltpu.VMEM((peers, 3 * rows, LANES), jnp.float32),
            pltpu.VMEM((height, 3 * sizes[2]), jnp.bfloat16),
            pltpu.VMEM((3 * sizes[2], rows * LANES), jnp.bfloat16),
            pltpu.VMEM((height, rows * LANES), jnp.float32),
            pltpu.VMEM((3 * slots_high, LANES), jnp.float32),
            pltpu.VMEM((3 * slots_high, 2 * LANES), jnp.bfloat16),
            pltpu.SemaphoreType.DMA((peers,)),
            pltpu.SemaphoreType.DMA((peers,)),
        ],
        compiler_params=pltpu.CompilerParams(
            vmem_limit_bytes=VMEM_LIMIT, collective_id=1, has_side_effects=True
        ),
        name="homeward",
    )(position, velocity, slots)


def shards(populations, displacement, stiffness, base_node, offset, destination):
    size_x, size_y, size_z = (populations.shape[1], populations.shape[2], populations.shape[3])
    peer_count = lax.axis_size(("gz", "gy"))
    markers = displacement.shape[1]
    capacity = max(2, (2 * markers + peer_count - 1) // peer_count)
    rows = -(-capacity // LANES)
    chunks = -(-markers // LANES)
    spare = chunks * LANES - markers
    sizes = (size_x, size_y, size_z)
    forces = marker_forces(displacement, stiffness)
    position = base_node.astype(jnp.float32) + offset
    target = jnp.pad(destination[:, 0], (0, spare), constant_values=-1).reshape(chunks, LANES)
    payload = jnp.pad(jnp.concatenate([forces, position], axis=0), ((0, 0), (0, spare)))
    field, slots, marker_position = outward(target, payload, peer_count, rows, sizes)
    force_field = field.reshape(3, size_x, size_y, size_z)
    new_populations, velocity = fluid(populations, force_field)
    velocity = velocity.reshape(3 * size_x * size_y, size_z)
    marker_velocity = homeward(marker_position, velocity, slots, markers, rows, sizes)
    return (new_populations, marker_velocity)


def solution(mesh):
    return jax.shard_map(
        shards,
        mesh=mesh,
        in_specs=(
            P(None, ("groups", "gx"), "gy", "gz"),
            P(None, ("groups", "gz", "gy", "gx")),
            P(("groups", "gz", "gy", "gx")),
            P(None, ("groups", "gz", "gy", "gx")),
            P(None, ("groups", "gz", "gy", "gx")),
            P(("groups", "gz", "gy", "gx"), None),
        ),
        out_specs=(P(None, ("groups", "gx"), "gy", "gz"), P(None, ("groups", "gz", "gy", "gx"))),
        check_vma=False,
    )
```
